128 devices in a mesh: group: 16 (over x, z_hi, core), head: 8 (over y, z_lo).
Axes of the slice: x: 4, y: 4, z: 4 (z_hi: 2, z_lo: 2; z = z_hi * 2 + z_lo), core: 2. Of those that a mesh axis runs over, the one named last changes fastest.
Arguments:
- queries: bfloat16 [4096, 5120], P('group', 'head'), may hold values from -8 to 8
- keys: bfloat16 [4096, 5120], P('group', 'head'), may hold values from -6 to 6
- values: bfloat16 [4096, 5120], P('group', 'head'), may hold values from -6 to 6
- text_keys: bfloat16 [512, 5120], P(None, 'head'), may hold values from -8 to 8
- text_values: bfloat16 [512, 5120], P(None, 'head'), may hold values from -6 to 6
- d_out: bfloat16 [4096, 5120], P('group', 'head'), may hold values from -6 to 6
- gain_q: bfloat16 [5120], P('head'), may hold values from 0.099609375 to 1.8984375
- gain_k: bfloat16 [5120], P('head'), may hold values from 0.099609375 to 1.8984375
- group_of: int32 [16], replicated, may hold values from 0 to 15, each once
Outputs:
- d_queries: bfloat16 [4096, 5120], P('group', 'head')
- d_keys: bfloat16 [4096, 5120], P('group', 'head')
- d_values: bfloat16 [4096, 5120], P('group', 'head')
- d_text_keys: bfloat16 [512, 5120], P(None, 'head')
- d_text_values: bfloat16 [512, 5120], P(None, 'head')
The draws below stay inside these ranges and needn't reach their ends.
Inputs may be any that keep to these rules, and one draw needn't show every extreme that they name: `group_of`: each group number appears once.
All inputs are finite; a program needn't handle non-finite values.
Results may differ from the reference program's by a relative error of at most 0.014.
The reference program's roundings to bfloat16 on the way (of `soft`, `out` and `ds`) count: a program that leaves them out, or rounds other values in their place, can miss the bound.
Values may be sent and summed in bfloat16 or wider, within the bound.
A program may use at most 128 MiB of HBM per device.

```python
import jax
import jax.numpy as jnp
from jax import lax

DH = 128
TEXT = 512
GROUP_TOK = 256
HEADS = 40
TOKENS = 4096
N_GROUP = 16


def draw_text_keys(key, part):
    key = jax.random.fold_in(key, 11)
    base = jnp.clip(jax.random.normal(key, (TEXT, HEADS * DH), jnp.float32), -6.0, 6.0)
    return base.astype(jnp.bfloat16)


def draw_queries(key, part):
    key = jax.random.fold_in(key, 12)
    fresh = jnp.clip(jax.random.normal(key, (TOKENS, HEADS * DH), jnp.float32), -6.0, 6.0)
    return fresh.astype(jnp.bfloat16)


def steps_of(key, extent, split, least, top_value):
    loudness, own = 1.0, jax.random.fold_in(key, 6)
    for position, blocks in split:
        heights = jnp.exp(jax.random.uniform(jax.random.fold_in(own, position), (blocks,), jnp.float32, least / len(split), top_value / len(split)))
        loudness = loudness * jnp.repeat(heights, extent[position] // blocks).reshape([-1 if axis == position else 1 for axis in range(len(extent))])
    return loudness


def bell_draw(key, shape, scale, bound, pieces=(), kind=jnp.bfloat16):
    values = jax.random.normal(key, shape, jnp.float32) * scale
    if len(pieces) > 0:
        values = steps_of(key, shape, pieces, -0.22, 0.18) * values
    return jnp.clip(values, min=-bound, max=bound).astype(kind)


def setup_inputs(seed: int = 0) -> dict:
    arg_keys = jax.random.split(jax.random.key(seed), 10)
    queries = draw_queries(jax.random.fold_in(arg_keys[9], 71), 0)
    keys = bell_draw(arg_keys[1], (TOKENS, HEADS * DH), 1.0, 6.0, ((0, 16), (1, 8)))
    values = bell_draw(arg_keys[2], (TOKENS, HEADS * DH), 1.0, 6.0, ((0, 16), (1, 8)))
    text_keys = draw_text_keys(jax.random.fold_in(arg_keys[9], 71), 0)
    text_values = bell_draw(arg_keys[4], (TEXT, HEADS * DH), 1.0, 6.0, ((1, 8),))
    d_out = bell_draw(arg_keys[5], (TOKENS, HEADS * DH), 1.0, 6.0, ((0, 16), (1, 8)))
    gain_q = jnp.clip(1.0 + 0.18 * jax.random.normal(arg_keys[6], (HEADS * DH,), jnp.float32), 0.099609375, 1.8984375).astype(jnp.bfloat16)
    gain_k = jnp.clip(1.0 + 0.18 * jax.random.normal(arg_keys[7], (HEADS * DH,), jnp.float32), 0.099609375, 1.8984375).astype(jnp.bfloat16)
    group_of = jax.random.permutation(arg_keys[8], N_GROUP).astype(jnp.int32)
    return {"queries": queries, "keys": keys, "values": values, "text_keys": text_keys, "text_values": text_values, "d_out": d_out, "gain_q": gain_q, "gain_k": gain_k, "group_of": group_of}


EPS = 1e-06

def rms_scale(x):
    return lax.rsqrt(lax.optimization_barrier(jnp.mean(x * x, axis=-1)) + EPS)

def reference(queries, keys, values, text_keys, text_values, d_out, gain_q, gain_k, group_of):
    rows = queries.shape[0]
    width = queries.shape[1]
    heads = width // DH
    scale = DH ** (-0.5)
    q_float = queries.astype(jnp.float32)
    k_float = keys.astype(jnp.float32)
    scale_q = rms_scale(q_float)
    scale_k = rms_scale(k_float)
    gains_q = gain_q.astype(jnp.float32)
    gains_k = gain_k.astype(jnp.float32)
    q_norm = (q_float * scale_q[:, None] * gains_q).astype(jnp.bfloat16)
    k_norm = (k_float * scale_k[:, None] * gains_k).astype(jnp.bfloat16)
    row_group = group_of[jnp.arange(rows) // GROUP_TOK]
    visible = jnp.concatenate([row_group[None, :] <= row_group[:, None], jnp.ones((rows, TEXT), bool)], axis=1)

    def heads_first(x):
        return x.reshape(x.shape[0], heads, DH).transpose(1, 0, 2)

    def heads_last(x):
        return x.transpose(1, 0, 2).reshape(x.shape[1], width)
    key_set = jnp.concatenate([k_norm, text_keys], axis=0)
    value_set = jnp.concatenate([values, text_values], axis=0)

    def one_head(items):
        qh, kh, vh, gh = items
        s = jnp.dot(qh, kh.T, preferred_element_type=jnp.float32) * scale
        s = jnp.where(visible, s, -jnp.inf)
        top = lax.optimization_barrier(jnp.max(s, axis=-1, keepdims=True))
        lse = top + jnp.log(lax.optimization_barrier(jnp.sum(jnp.exp(s - top), axis=-1, keepdims=True)))
        p = jnp.exp(s - lse)
        soft = p.astype(jnp.bfloat16)
        out = lax.optimization_barrier(jnp.dot(soft, vh, preferred_element_type=jnp.float32).astype(jnp.bfloat16))
        delta = lax.optimization_barrier(jnp.sum(gh.astype(jnp.float32) * out.astype(jnp.float32), axis=-1, keepdims=True))
        dp = jnp.dot(gh, vh.T, preferred_element_type=jnp.float32)
        ds = (p * (dp - delta) * scale).astype(jnp.bfloat16)
        gq = jnp.dot(ds, kh, preferred_element_type=jnp.float32)
        gk = jnp.dot(ds.T, qh, preferred_element_type=jnp.float32)
        gv = jnp.dot(soft.T, gh, preferred_element_type=jnp.float32)
        return (gq, gk, gv)
    gq, gk, gv = lax.map(one_head, (heads_first(q_norm), heads_first(key_set), heads_first(value_set), heads_first(d_out)))
    dq_norm = heads_last(gq)
    dk_norm = heads_last(gk[:, :rows])
    d_values = heads_last(gv[:, :rows]).astype(jnp.bfloat16)
    d_text_keys = heads_last(gk[:, rows:]).astype(jnp.bfloat16)
    d_text_values = heads_last(gv[:, rows:]).astype(jnp.bfloat16)
    grad_q = dq_norm * gains_q
    grad_k = dk_norm * gains_k
    d_queries = scale_q[:, None] * grad_q - q_float * (scale_q ** 3 * lax.optimization_barrier(jnp.mean(q_float * grad_q, axis=-1)))[:, None]
    d_keys = scale_k[:, None] * grad_k - k_float * (scale_k ** 3 * lax.optimization_barrier(jnp.mean(k_float * grad_k, axis=-1)))[:, None]
    return (d_queries.astype(jnp.bfloat16), d_keys.astype(jnp.bfloat16), d_values, d_text_keys, d_text_values)
```

```python
import functools
import math

import jax
import jax.numpy as jnp
from jax import lax
from jax.experimental import pallas as pl
from jax.experimental.pallas import tpu as pltpu
from jax.sharding import PartitionSpec as P

DH = 128
EPS = 1e-06
BLK = 256
NG = 16
NH = 5
NDEV = 15
WIN = 96
ROWS = 1408
QPAD = 1552
TWIN = 176
SCALE = DH ** (-0.5)
MESH = pl.DeviceIdType.MESH
F32 = jnp.float32
BF16 = jnp.bfloat16
VMEM_LIMIT = 56 * 1024 * 1024


def greet(me, hd, nh):
    barrier = pltpu.get_barrier_semaphore()
    for d in range(1, NG):
        pl.semaphore_signal(
            barrier, inc=1, device_id={"group": lax.rem(me + d, NG)}, device_id_type=MESH
        )
    for d in range(1, nh):
        pl.semaphore_signal(
            barrier, inc=1, device_id={"head": lax.rem(hd + d, nh)}, device_id_type=MESH
        )
    pl.semaphore_wait(barrier, NG - 1 + nh - 1)


def row_sums(acc):
    return jnp.sum(acc.T, axis=0, keepdims=True)


def as_column(row):
    return jnp.broadcast_to(row, (DH, BLK)).T


def head_sum(row_q, row_k, send, recv, send_sem, recv_sem, hd, nh):
    send[...] = jnp.concatenate([row_q, row_k, jnp.zeros((6, BLK), F32)], axis=0)
    copies = []
    for d in range(1, nh):
        peer = lax.rem(hd + d, nh)
        copy = pltpu.make_async_remote_copy(
            src_ref=send,
            dst_ref=recv.at[d],
            send_sem=send_sem.at[d],
            recv_sem=recv_sem.at[d],
            device_id={"head": peer},
            device_id_type=MESH,
        )
        copy.start()
        copies.append(copy)
    return copies


def head_total(copies, send, recv, nh):
    for copy in copies:
        copy.wait()
    total = send[...]
    for d in range(1, nh):
        total = total + recv[d]
    return total


def spread_kernel(
    nh, q_ref, k_ref, v_ref, g_ref, gain_q, gain_k,
    kall, vall, qall, gall, scales,
    qn, kn, sq_send, sq_recv, send_sem, recv_sem, local_sem, ss, rs,
):
    me = lax.axis_index("group")
    hd = lax.axis_index("head")
    greet(me, hd, nh)

    def whole(ref, out, kind, t):
        head = lax.div(t, 3)
        cols = pl.ds(pl.multiple_of(head * DH, DH), DH)
        return ref.at[:, cols], out.at[pl.ds(pl.multiple_of(me * BLK, BLK), BLK)]

    def third(ref, out, kind, t):
        head = lax.div(t, 3)
        part = lax.rem(t, 3)
        cols = pl.ds(pl.multiple_of(head * DH, DH), DH)
        src = ref.at[pl.ds(pl.multiple_of(part * 80, 16), WIN), cols]
        return src, out.at[pl.ds(pl.multiple_of(me * WIN, WIN), WIN)]

    plan = ((whole, v_ref, vall), (third, g_ref, gall), (whole, kn, kall), (third, qn, qall))

    def remote(kind, t):
        form, ref, out = plan[kind]
        src, dst = form(ref, out, kind, t)
        return pltpu.make_async_remote_copy(
            src_ref=src,
            dst_ref=dst,
            send_sem=send_sem.at[kind, t],
            recv_sem=recv_sem.at[kind, me],
            device_id={"group": t},
            device_id_type=MESH,
        )

    def local(kind):
        form, ref, out = plan[kind]
        src, dst = form(ref, out, kind, me)
        return pltpu.make_async_copy(src, dst, local_sem.at[kind])

    def send_all(kinds):
        @pl.loop(1, NG)
        def _(d):
            t = lax.rem(me + d, NG)

            @pl.when(t < NDEV)
            def _():
                for kind in kinds:
                    remote(kind, t).start()

        @pl.when(me < NDEV)
        def _():
            for kind in kinds:
                local(kind).start()

    acc_q = jnp.zeros((BLK, DH), F32)
    acc_k = jnp.zeros((BLK, DH), F32)
    for h in range(NH):
        cols = slice(h * DH, (h + 1) * DH)
        x = q_ref[:, cols].astype(F32)
        acc_q = acc_q + x * x
        x = k_ref[:, cols].astype(F32)
        acc_k = acc_k + x * x
    copies = head_sum(row_sums(acc_q), row_sums(acc_k), sq_send, sq_recv, ss, rs, hd, nh)
    send_all((0, 1))
    total = head_total(copies, sq_send, sq_recv, nh)
    scale = lax.rsqrt(total / (NH * DH * nh) + EPS)
    scales[...] = scale
    col_q = as_column(scale[0:1])
    col_k = as_column(scale[1:2])
    for h in range(NH):
        cols = slice(h * DH, (h + 1) * DH)
        kn[:, cols] = (k_ref[:, cols].astype(F32) * col_k * gain_k[:, cols].astype(F32)).astype(BF16)
        qn[:, cols] = (q_ref[:, cols].astype(F32) * col_q * gain_q[:, cols].astype(F32)).astype(BF16)
    send_all((2, 3))

    @pl.loop(1, NG)
    def _(d):
        t = lax.rem(me + d, NG)

        @pl.when(t < NDEV)
        def _():
            for kind in range(4):
                remote(kind, t).wait_send()

        @pl.when(me < NDEV)
        def _():
            for kind in range(4):
                form, ref, out = plan[kind]
                rows = BLK if kind in (0, 2) else WIN
                dst = out.at[pl.ds(pl.multiple_of(t * rows, rows), rows)]
                pltpu.make_async_remote_copy(
                    src_ref=dst,
                    dst_ref=dst,
                    send_sem=send_sem.at[kind, t],
                    recv_sem=recv_sem.at[kind, t],
                    device_id={"group": t},
                    device_id_type=MESH,
                ).wait_recv()

    @pl.when(me < NDEV)
    def _():
        for kind in range(4):
            local(kind).wait()


def attend_kernel(
    meta, kall, vall, qall, gall, tk_any, tv_any,
    gk_out, gv_out, gq_out, tk_out, tv_out,
    ks, vs, kt, qs, gs, s_buf, d_buf, p_buf, ds_buf, dq_acc, dq_buf, order, offs, sem,
):
    me = meta[NG]

    @pl.when(me < NDEV)
    def _():
        head = lax.div(me, 3)
        part = lax.rem(me, 3)
        cols = pl.ds(pl.multiple_of(head * DH, DH), DH)
        copy_k = pltpu.make_async_copy(tk_any.at[:, cols], ks.at[pl.ds(0, 2 * BLK)], sem.at[0])
        copy_v = pltpu.make_async_copy(tv_any.at[:, cols], vs.at[pl.ds(0, 2 * BLK)], sem.at[1])
        copy_k.start()
        copy_v.start()
        for s in range(NG):
            order[meta[s]] = s
        at = 0
        for r in range(NG):
            s = order[r]
            c = lax.rem(s, 3)
            offs[r] = at
            src = pl.multiple_of(s * WIN + jnp.where(part > c, 16, 0), 16)
            at = pl.multiple_of(at, 16) if r else 0
            qs[pl.ds(at, WIN), :] = qall[pl.ds(src, WIN), :]
            gs[pl.ds(at, WIN), :] = gall[pl.ds(src, WIN), :]
            at = at + jnp.where(part == c, 96, 80)
            rows = pl.ds(pl.multiple_of(s * BLK, BLK), BLK)
            ks[(r + 2) * BLK:(r + 3) * BLK, :] = kall[rows, :]
            vs[(r + 2) * BLK:(r + 3) * BLK, :] = vall[rows, :]
        at = pl.multiple_of(at, 16)
        qs[pl.ds(at, 48), :] = jnp.zeros((48, DH), BF16)
        gs[pl.ds(at, 48), :] = jnp.zeros((48, DH), BF16)
        copy_k.wait()
        copy_v.wait()

        @pl.loop(0, NG + 2)
        def _(ci):
            kt[ci] = ks[pl.ds(pl.multiple_of(ci * BLK, BLK), BLK), :].T

        def rank_at(row):
            rank = 0
            for r in range(1, NG):
                rank = rank + (row >= offs[r]).astype(jnp.int32)
            return rank

        def fold(x, op):
            return op(x.reshape(BLK // 8, 8, x.shape[-1]), axis=0)

        def rows_block(start, n):
            rows = pl.ds(start, n)
            qb = qs[rows, :]
            gb = gs[rows, :]
            low = rank_at(start)
            high = rank_at(start + n - 1)
            lanes = lax.broadcasted_iota(jnp.int32, (1, n), 1) + start
            row_rank = jnp.zeros((1, n), jnp.int32)
            for r in range(1, NG):
                row_rank = row_rank + (lanes >= offs[r]).astype(jnp.int32)

            def chunk(ci):
                return pl.ds(pl.multiple_of(ci * BLK, BLK), BLK)

            def scores(ci, top, masked):
                s = lax.dot_general(
                    ks[chunk(ci), :], qb, (((1,), (1,)), ((), ())), preferred_element_type=F32
                ) * (SCALE * math.log2(math.e))
                if masked:
                    s = jnp.where(row_rank >= ci - 2, s, -jnp.inf)
                s_buf[chunk(ci), 0:n] = s
                return jnp.maximum(top, fold(s, jnp.max))

            top = jnp.full((8, n), -jnp.inf, F32)
            top = lax.fori_loop(0, low + 3, lambda ci, t: scores(ci, t, False), top)
            top = lax.fori_loop(low + 3, high + 3, lambda ci, t: scores(ci, t, True), top)
            top = jnp.max(top, axis=0, keepdims=True)

            def weigh(ci, carry):
                e = jnp.exp2(s_buf[chunk(ci), 0:n] - top)
                dp = lax.dot_general(
                    vs[chunk(ci), :], gb, (((1,), (1,)), ((), ())), preferred_element_type=F32
                )
                s_buf[chunk(ci), 0:n] = e
                d_buf[chunk(ci), 0:n] = dp
                return carry[0] + fold(e, jnp.sum), carry[1] + fold(e * dp, jnp.sum)

            zero = jnp.zeros((8, n), F32)
            norm, inner = lax.fori_loop(0, high + 3, weigh, (zero, zero))
            inv = 1.0 / jnp.sum(norm, axis=0, keepdims=True)
            delta = jnp.sum(inner, axis=0, keepdims=True) * inv
            dq_acc[:, 0:n] = jnp.zeros((DH, n), F32)

            @pl.loop(0, high + 3)
            def _(ci):
                p = s_buf[chunk(ci), 0:n] * inv
                ds = (p * (d_buf[chunk(ci), 0:n] - delta) * SCALE).astype(BF16)
                p_buf[chunk(ci), rows] = p.astype(BF16)
                ds_buf[chunk(ci), rows] = ds
                dq_acc[:, 0:n] += jnp.dot(kt[ci], ds, preferred_element_type=F32)

            dq_buf[rows, :] = dq_acc[:, 0:n].T

        @pl.loop(0, 5)
        def _(b):
            rows_block(pl.multiple_of(b * BLK, BLK), BLK)

        rows_block(5 * BLK, 128)

        def grads(ci, first, put):
            keys = pl.ds(pl.multiple_of(ci * BLK, BLK), BLK)
            for b in range(6):
                @pl.when(first == b)
                def _():
                    rows = slice(b * BLK, ROWS)
                    put(
                        jnp.dot(ds_buf[keys, rows], qs[rows, :], preferred_element_type=F32),
                        jnp.dot(p_buf[keys, rows], gs[rows, :], preferred_element_type=F32),
                    )

        @pl.loop(0, 2)
        def _(ci):
            keys = pl.ds(pl.multiple_of(ci * BLK, BLK), BLK)
            rows = slice(0, ROWS)
            tk_out[keys, :] = jnp.dot(
                ds_buf[keys, rows], qs[rows, :], preferred_element_type=F32
            ).astype(BF16)
            tv_out[keys, :] = jnp.dot(
                p_buf[keys, rows], gs[rows, :], preferred_element_type=F32
            ).astype(BF16)

        @pl.loop(0, NG)
        def _(r):
            def put(gk, gv):
                place = pl.ds(pl.multiple_of(order[r] * BLK, BLK), BLK)
                gk_out[place, :] = gk.astype(BF16)
                gv_out[place, :] = gv.astype(BF16)

            grads(r + 2, lax.div(offs[r], BLK), put)
            src = pl.ds(pl.multiple_of(offs[r], 16), WIN)
            gq_out[pl.ds(pl.multiple_of(order[r] * WIN, WIN), WIN), :] = dq_buf[src, :].astype(BF16)


def text_start(part):
    return part * TWIN - 16 * (part // 2)


def return_kernel(
    nh, gk, gv, gq, tk, tv, q_ref, k_ref, gain_q, gain_k, scales,
    dq, dk, dv, dtk, dtv,
    got_k, got_v, got_q, text_in, text_sum, text_all, uq, uk, sq_send, sq_recv,
    send_sem, recv_sem, local_sem, trio_send, trio_recv, all_send, all_recv, ss, rs,
):
    me = lax.axis_index("group")
    hd = lax.axis_index("head")
    greet(me, hd, nh)
    part = lax.rem(me, 3)
    working = me < NDEV

    def trio(j, i):
        other = lax.rem(part + j, 3)
        start = pl.multiple_of(other * TWIN - 16 * lax.div(other, 2), 16)
        ref = (tk, tv)[i]
        return pltpu.make_async_remote_copy(
            src_ref=ref.at[pl.ds(start, TWIN)],
            dst_ref=text_in.at[j, i],
            send_sem=trio_send.at[j, i],
            recv_sem=trio_recv.at[j, i],
            device_id={"group": me - part + other},
            device_id_type=MESH,
        )

    def back(kind, t):
        ref, got = ((gk, got_k), (gv, got_v), (gq, got_q))[kind]
        n = (BLK, BLK, WIN)[kind]
        return ref.at[pl.ds(pl.multiple_of(t * n, n), n)], got.at[me]

    def back_remote(kind, t):
        src, dst = back(kind, t)
        return pltpu.make_async_remote_copy(
            src_ref=src,
            dst_ref=dst,
            send_sem=send_sem.at[kind, t],
            recv_sem=recv_sem.at[kind, me],
            device_id={"group": t},
            device_id_type=MESH,
        )

    def back_local(kind):
        src, dst = back(kind, me)
        return pltpu.make_async_copy(src, dst, local_sem.at[kind])

    def cast(t):
        return pltpu.make_async_remote_copy(
            src_ref=text_sum,
            dst_ref=text_all.at[me],
            send_sem=all_send.at[t],
            recv_sem=all_recv.at[me],
            device_id={"group": t},
            device_id_type=MESH,
        )

    @pl.when(working)
    def _():
        for j in (1, 2):
            for i in range(2):
                trio(j, i).start()

        @pl.loop(1, NG)
        def _(d):
            t = lax.rem(me + d, NG)
            for kind in range(3):
                back_remote(kind, t).start()

        for kind in range(3):
            back_local(kind).start()
        for j in (1, 2):
            for i in range(2):
                trio(j, i).wait()
        start = pl.multiple_of(part * TWIN - 16 * lax.div(part, 2), 16)
        for i in range(2):
            own = (tk, tv)[i][pl.ds(start, TWIN), :].astype(F32)
            text_sum[i] = (own + text_in[1, i].astype(F32) + text_in[2, i].astype(F32)).astype(BF16)

        @pl.loop(1, NG)
        def _(d):
            cast(lax.rem(me + d, NG)).start()

        text_all[me] = text_sum[...]
        for kind in range(3):
            back_local(kind).wait()

    @pl.loop(1, NG)
    def _(d):
        t = lax.rem(me + d, NG)

        @pl.when(t < NDEV)
        def _():
            for kind in range(3):
                got = (got_k, got_v, got_q)[kind]
                pltpu.make_async_remote_copy(
                    src_ref=got.at[t],
                    dst_ref=got.at[t],
                    send_sem=send_sem.at[kind, t],
                    recv_sem=recv_sem.at[kind, t],
                    device_id={"group": t},
                    device_id_type=MESH,
                ).wait_recv()

    acc_q = jnp.zeros((BLK, DH), F32)
    acc_k = jnp.zeros((BLK, DH), F32)
    c = lax.rem(me, 3)
    for h in range(NH):
        cols = slice(h * DH, (h + 1) * DH)
        for p in range(3):
            start = pl.multiple_of(p * 80 + jnp.where(p > c, 16, 0), 16)
            uq[pl.ds(start, WIN), cols] = got_q[3 * h + p].astype(F32) * gain_q[:, cols].astype(F32)
        u = got_k[3 * h].astype(F32) + got_k[3 * h + 1].astype(F32) + got_k[3 * h + 2].astype(F32)
        u = u * gain_k[:, cols].astype(F32)
        uk[:, cols] = u
        acc_k = acc_k + u * k_ref[:, cols].astype(F32)
        acc_q = acc_q + uq[0:BLK, cols] * q_ref[:, cols].astype(F32)
    copies = head_sum(row_sums(acc_q), row_sums(acc_k), sq_send, sq_recv, ss, rs, hd, nh)
    for h in range(NH):
        cols = slice(h * DH, (h + 1) * DH)
        dv[:, cols] = (
            got_v[3 * h].astype(F32) + got_v[3 * h + 1].astype(F32) + got_v[3 * h + 2].astype(F32)
        ).astype(BF16)
    inner = head_total(copies, sq_send, sq_recv, nh) / (NH * DH * nh)
    scale = scales[...]
    cube = scale * scale * scale * inner
    for row, u_ref, x_ref, out in ((0, uq, q_ref, dq), (1, uk, k_ref, dk)):
        col = as_column(scale[row:row + 1])
        col3 = as_column(cube[row:row + 1])
        for h in range(NH):
            cols = slice(h * DH, (h + 1) * DH)
            out[:, cols] = (col * u_ref[0:BLK, cols] - x_ref[:, cols].astype(F32) * col3).astype(BF16)

    @pl.loop(1, NG)
    def _(d):
        t = lax.rem(me + d, NG)

        @pl.when(t < NDEV)
        def _():
            pltpu.make_async_remote_copy(
                src_ref=text_all.at[t],
                dst_ref=text_all.at[t],
                send_sem=all_send.at[t],
                recv_sem=all_recv.at[t],
                device_id={"group": t},
                device_id_type=MESH,
            ).wait_recv()

    for i in range(NDEV):
        cols = slice((i // 3) * DH, (i // 3 + 1) * DH)
        rows = slice(text_start(i % 3), text_start(i % 3) + TWIN)
        dtk[rows, cols] = text_all[i, 0]
        dtv[rows, cols] = text_all[i, 1]

    @pl.when(working)
    def _():
        @pl.loop(1, NG)
        def _(d):
            t = lax.rem(me + d, NG)
            for kind in range(3):
                back_remote(kind, t).wait_send()
            cast(t).wait_send()


VM = pl.BlockSpec(memory_space=pltpu.VMEM)
SM = pl.BlockSpec(memory_space=pltpu.SMEM)
ANY = pl.BlockSpec(memory_space=pl.ANY)
DMA = pltpu.SemaphoreType.DMA


def shape(dims, dtype=BF16):
    return jax.ShapeDtypeStruct(dims, dtype)


def body(nh, queries, keys, values, text_keys, text_values, d_out, gain_q, gain_k, group_of):
    gain_q = gain_q[None, :]
    gain_k = gain_k[None, :]
    kall, vall, qall, gall, scales = pl.pallas_call(
        functools.partial(spread_kernel, nh),
        out_shape=(
            shape((NG * BLK, DH)), shape((NG * BLK, DH)), shape((QPAD, DH)), shape((QPAD, DH)),
            shape((8, BLK), F32),
        ),
        in_specs=[VM] * 6,
        out_specs=(ANY, ANY, ANY, ANY, VM),
        scratch_shapes=[
            pltpu.VMEM((BLK, NH * DH), BF16),
            pltpu.VMEM((BLK, NH * DH), BF16),
            pltpu.VMEM((8, BLK), F32),
            pltpu.VMEM((nh, 8, BLK), F32),
            DMA((4, NG)), DMA((4, NG)), DMA((4,)), DMA((nh,)), DMA((nh,)),
        ],
        compiler_params=pltpu.CompilerParams(
            collective_id=0, has_side_effects=True, vmem_limit_bytes=VMEM_LIMIT
        ),
        name="spread",
    )(queries, keys, values, d_out, gain_q, gain_k)

    meta = jnp.concatenate([group_of, lax.axis_index("group")[None].astype(jnp.int32)])
    gk, gv, gq, tk, tv = pl.pallas_call(
        attend_kernel,
        out_shape=(
            shape((NG * BLK, DH)), shape((NG * BLK, DH)), shape((NG * WIN, DH)),
            shape((2 * BLK, DH)), shape((2 * BLK, DH)),
        ),
        in_specs=[SM, VM, VM, VM, VM, ANY, ANY],
        out_specs=(VM,) * 5,
        scratch_shapes=[
            pltpu.VMEM(((NG + 2) * BLK, DH), BF16),
            pltpu.VMEM(((NG + 2) * BLK, DH), BF16),
            pltpu.VMEM((NG + 2, DH, BLK), BF16),
            pltpu.VMEM((ROWS + 32, DH), BF16),
            pltpu.VMEM((ROWS + 32, DH), BF16),
            pltpu.VMEM(((NG + 2) * BLK, BLK), F32),
            pltpu.VMEM(((NG + 2) * BLK, BLK), F32),
            pltpu.VMEM(((NG + 2) * BLK, ROWS), BF16),
            pltpu.VMEM(((NG + 2) * BLK, ROWS), BF16),
            pltpu.VMEM((DH, BLK), F32),
            pltpu.VMEM((ROWS + 32, DH), F32),
            pltpu.SMEM((NG,), jnp.int32),
            pltpu.SMEM((NG,), jnp.int32),
            DMA((2,)),
        ],
        compiler_params=pltpu.CompilerParams(vmem_limit_bytes=VMEM_LIMIT),
        name="attend",
    )(meta, kall, vall, qall, gall, text_keys, text_values)

    return pl.pallas_call(
        functools.partial(return_kernel, nh),
        out_shape=(
            shape((BLK, NH * DH)), shape((BLK, NH * DH)), shape((BLK, NH * DH)),
            shape((2 * BLK, NH * DH)), shape((2 * BLK, NH * DH)),
        ),
        in_specs=[ANY, ANY, ANY] + [VM] * 7,
        out_specs=(VM,) * 5,
        scratch_shapes=[
            pltpu.VMEM((NDEV, BLK, DH), BF16),
            pltpu.VMEM((NDEV, BLK, DH), BF16),
            pltpu.VMEM((NDEV, WIN, DH), BF16),
            pltpu.VMEM((3, 2, TWIN, DH), BF16),
            pltpu.VMEM((2, TWIN, DH), BF16),
            pltpu.VMEM((NG, 2, TWIN, DH), BF16),
            pltpu.VMEM((BLK + 16, NH * DH), F32),
            pltpu.VMEM((BLK, NH * DH), F32),
            pltpu.VMEM((8, BLK), F32),
            pltpu.VMEM((nh, 8, BLK), F32),
            DMA((3, NG)), DMA((3, NG)), DMA((3,)), DMA((3, 2)), DMA((3, 2)), DMA((NG,)), DMA((NG,)),
            DMA((nh,)), DMA((nh,)),
        ],
        compiler_params=pltpu.CompilerParams(
            collective_id=1, has_side_effects=True, vmem_limit_bytes=VMEM_LIMIT
        ),
        name="give_back",
    )(gk, gv, gq, tk, tv, queries, keys, gain_q, gain_k, scales)


def solution(mesh):
    placed = (
        P("group", "head"),
        P("group", "head"),
        P("group", "head"),
        P(None, "head"),
        P(None, "head"),
        P("group", "head"),
        P("head"),
        P("head"),
        P(),
    )
    return jax.shard_map(
        functools.partial(body, mesh.shape["head"]),
        mesh=mesh,
        in_specs=placed,
        out_specs=(
            P("group", "head"),
            P("group", "head"),
            P("group", "head"),
            P(None, "head"),
            P(None, "head"),
        ),
        check_vma=False,
    )
```

```python
import functools
import math

import jax
import jax.numpy as jnp
from jax import lax
from jax.experimental import pallas as pl
from jax.experimental.pallas import tpu as pltpu
from jax.sharding import PartitionSpec as P

DH = 128
EPS = 1e-06
BLK = 256
NG = 16
NH = 5
NDEV = 15
KC = 512
NP = 9
ROWS = 1536
SCALE = DH ** (-0.5)
LOG = SCALE * math.log2(math.e)
MESH = pl.DeviceIdType.MESH
F32 = jnp.float32
BF16 = jnp.bfloat16
VMEM_LIMIT = 62 * 1024 * 1024


def greet(me, hd, nh):
    barrier = pltpu.get_barrier_semaphore()
    for d in range(1, NG):
        pl.semaphore_signal(
            barrier, inc=1, device_id={"group": lax.rem(me + d, NG)}, device_id_type=MESH
        )
    for d in range(1, nh):
        pl.semaphore_signal(
            barrier, inc=1, device_id={"head": lax.rem(hd + d, nh)}, device_id_type=MESH
        )
    pl.semaphore_wait(barrier, NG - 1 + nh - 1)


def row_sums(acc):
    return jnp.sum(acc.T, axis=0, keepdims=True)


def as_column(row):
    return jnp.broadcast_to(row, (DH, BLK)).T


def head_sum(row_q, row_k, send, recv, send_sem, recv_sem, hd, nh):
    send[...] = jnp.concatenate([row_q, row_k, jnp.zeros((6, BLK), F32)], axis=0)
    copies = []
    for d in range(1, nh):
        peer = lax.rem(hd + d, nh)
        copy = pltpu.make_async_remote_copy(
            src_ref=send,
            dst_ref=recv.at[d],
            send_sem=send_sem.at[d],
            recv_sem=recv_sem.at[d],
            device_id={"head": peer},
            device_id_type=MESH,
        )
        copy.start()
        copies.append(copy)
    return copies


def head_total(copies, send, recv, nh):
    for copy in copies:
        copy.wait()
    total = send[...]
    for d in range(1, nh):
        total = total + recv[d]
    return total


def roles(t):
    h = lax.div(t, 3)
    odd = lax.rem(h, 2)
    return h, t - 3 * h, 3 * h + odd, 3 * h + 2 - 2 * odd


def push(src, dst, send_sem, recv_sem, t):
    return pltpu.make_async_remote_copy(
        src_ref=src, dst_ref=dst, send_sem=send_sem, recv_sem=recv_sem,
        device_id={"group": t}, device_id_type=MESH,
    )


def await_recv(dst, send_sem, recv_sem, t):
    push(dst, dst, send_sem, recv_sem, t).wait_recv()


def head_cols(h):
    return pl.ds(pl.multiple_of(h * DH, DH), DH)


def block(i, n):
    return pl.ds(pl.multiple_of(i * n, n), n)


def by_third(part, run):
    pl.when(part == 0)(lambda: run(96))
    pl.when(part > 0)(lambda: run(80))


def attend_kernel(
    nh, q_ref, k_ref, v_ref, g_ref, tk_ref, tv_ref, gain_q_ref, gain_k_ref, group_of, order,
    dq, dk, dv, dtk, dtv,
    qn, kn, kall, vall, qall, gall, ks, vs, kt, qs, gs, s_buf, d_buf, p_buf, ds_buf, dq_buf, dq_rank,
    tk, tv, pair_in, pair_sum, got, got_q, text_in, text_sum, text_all, uq, uk, sq_send, sq_recv,
    in_send, in_recv, relay_sem, local_sem, text_sem,
    pair_send, pair_recv, out_send, out_recv, q_send, q_recv, q_local,
    text_send, text_recv, cast_send, cast_recv, relay_send, mate_send, ss, rs,
):
    me = lax.axis_index("group")
    hd = lax.axis_index("head")
    core = lax.rem(me, 2)
    mate = me + 1 - 2 * core
    mirror = me + 2 - 4 * lax.rem(lax.div(me, 2), 2)
    my_head, my_part, my_pair, my_single = roles(me)
    working = me < NDEV
    alone = working & (me == my_single)
    paired = working & (me != my_single)
    size = jnp.where(my_part == 0, 96, 80)
    blocks = jnp.where(my_part == 0, 6, 5)
    gain_q = gain_q_ref[...].astype(F32)[None, :]
    gain_k = gain_k_ref[...].astype(F32)[None, :]

    def text_copy(i):
        return pltpu.make_async_copy(
            (tk_ref, tv_ref)[i].at[:, head_cols(my_head)], (ks, vs)[i].at[pl.ds(0, KC)],
            text_sem.at[i])

    pl.when(working)(lambda: [text_copy(i).start() for i in range(2)] and None)
    greet(me, hd, nh)

    whole = ((0, v_ref, vall), (2, kn, kall))
    thirds = ((1, g_ref, gall), (3, qn, qall))

    def third_src(ref, h, part, size):
        start = 0 if size == 96 else pl.multiple_of(part * 80 + 16, 16)
        return ref.at[pl.ds(start, size), head_cols(h)]

    def to_all(stage, act):
        kind, ref, out = whole[stage]
        kind3, ref3, out3 = thirds[stage]

        @pl.loop(1, NG)
        def _(d):
            t = lax.rem(me + d, NG)

            @pl.when(t < NDEV)
            def _():
                h, part, pair, single = roles(t)

                @pl.when((t == single) | (t == pair + core))
                def _():
                    act(push(ref.at[:, head_cols(h)], out.at[me],
                             in_send.at[kind, t], in_recv.at[kind, me], t))

                by_third(part, lambda size: act(
                    push(third_src(ref3, h, part, size), out3.at[me, pl.ds(0, size)],
                         in_send.at[kind3, t], in_recv.at[kind3, me], t)))

    def to_self(stage, act):
        kind, ref, out = whole[stage]
        kind3, ref3, out3 = thirds[stage]

        @pl.when(working)
        def _():
            act(pltpu.make_async_copy(
                ref.at[:, head_cols(my_head)], out.at[me], local_sem.at[kind]))
            by_third(my_part, lambda size: act(pltpu.make_async_copy(
                third_src(ref3, my_head, my_part, size), out3.at[me, pl.ds(0, size)],
                local_sem.at[kind3])))

    def start(copy):
        copy.start()

    def relay(stage, s):
        kind, ref, out = whole[stage]
        view = out.at[s]
        return push(view, view, relay_sem.at[kind, s], in_recv.at[kind, s], mate)

    def relay_all(stage):
        kind, ref, out = whole[stage]

        @pl.when(paired)
        def _():
            relay(stage, me).start()

            @pl.loop(1, 8)
            def _(d):
                s = lax.rem(me + NG - 2 * d, NG)
                await_recv(out.at[s], in_send.at[kind, s], in_recv.at[kind, s], s)
                relay(stage, s).start()

    acc_q = jnp.zeros((BLK, DH), F32)
    acc_k = jnp.zeros((BLK, DH), F32)
    for h in range(NH):
        cols = slice(h * DH, (h + 1) * DH)
        x = q_ref[:, cols].astype(F32)
        acc_q = acc_q + x * x
        x = k_ref[:, cols].astype(F32)
        acc_k = acc_k + x * x
    copies = head_sum(row_sums(acc_q), row_sums(acc_k), sq_send.at[0], sq_recv.at[0], ss.at[0], rs.at[0], hd, nh)
    to_all(0, start)
    to_self(0, start)
    total = head_total(copies, sq_send.at[0], sq_recv.at[0], nh)
    scale = lax.rsqrt(total / (NH * DH * nh) + EPS)
    col_q = as_column(scale[0:1])
    col_k = as_column(scale[1:2])
    for h in range(NH):
        cols = slice(h * DH, (h + 1) * DH)
        kn[:, cols] = (k_ref[:, cols].astype(F32) * col_k * gain_k[:, cols]).astype(BF16)
        qn[:, cols] = (q_ref[:, cols].astype(F32) * col_q * gain_q[:, cols]).astype(BF16)
    to_all(1, start)
    to_self(1, start)

    @pl.loop(0, blocks)
    def _(b):
        @pl.loop(lax.div(lax.div(b * BLK + BLK - 1, size), 2) + 2, NP)
        def _(i):
            for j in range(2):
                p_buf[b, 2 * i + j] = jnp.zeros((BLK, BLK), BF16)
                ds_buf[b, 2 * i + j] = jnp.zeros((BLK, BLK), BF16)

    to_self(0, lambda copy: copy.wait())
    relay_all(0)
    to_self(1, lambda copy: copy.wait())
    relay_all(1)

    @pl.when(working)
    def _():
        @pl.loop(1, NG)
        def _(d):
            s = lax.rem(me + d, NG)
            for kind, ref, out in whole:
                @pl.when((me == my_single) | (lax.rem(d, 2) == 1))
                def _():
                    await_recv(
                        out.at[s], in_send.at[kind, s], in_recv.at[kind, s], s)
            for kind, ref, out in thirds:
                by_third(my_part, lambda size: await_recv(
                    out.at[s, pl.ds(0, size)], in_send.at[kind, s], in_recv.at[kind, s], s))

    @pl.when(paired)
    def _():
        @pl.loop(0, 8)
        def _(d):
            s = lax.rem(me + 2 * d, NG)
            for stage in range(2):
                relay(stage, s).wait_send()

    for stage in range(2):
        to_all(stage, lambda copy: copy.wait_send())

    @pl.when(working)
    def _():
        for i in range(2):
            text_copy(i).wait()

        def gather(n):
            for r in range(NG):
                qs[r * n:(r + 1) * n, :] = qall[order[r], 0:n, :]
                gs[r * n:(r + 1) * n, :] = gall[order[r], 0:n, :]

        by_third(my_part, gather)
        for r in range(NG):
            ks[(r + 2) * BLK:(r + 3) * BLK, :] = kall[order[r]]
            vs[(r + 2) * BLK:(r + 3) * BLK, :] = vall[order[r]]
        for i in range(NP):
            kt[i] = ks[i * KC:(i + 1) * KC, :].T

        def fold(x, op):
            return op(x.reshape(x.shape[0] // 8, 8, x.shape[-1]), axis=0)

        def rows_block(blk, start, n):
            rows = pl.ds(start, BLK)
            q_cols = qs[rows, :].T
            g_cols = gs[rows, :].T
            lanes = lax.broadcasted_iota(jnp.int32, (1, BLK), 1) + start
            row_rank = jnp.zeros((1, BLK), jnp.int32)
            for r in range(1, NG):
                row_rank = row_rank + (lanes >= r * size).astype(jnp.int32)
            at = [slice(i * KC, (i + 1) * KC) for i in range(n)]
            top = jnp.full((1, BLK), -jnp.inf, F32)
            norm = jnp.zeros((8, BLK), F32)
            inner = jnp.zeros((8, BLK), F32)
            tops = []
            for i in range(n):
                s = jnp.dot(ks[at[i], :], q_cols, preferred_element_type=F32)
                dp = jnp.dot(vs[at[i], :], g_cols, preferred_element_type=F32)
                if i > max(0, (n - 1) - 3):
                    s = jnp.concatenate(
                        [
                            jnp.where(row_rank >= 2 * i - 2, s[0:BLK], -jnp.inf),
                            jnp.where(row_rank >= 2 * i - 1, s[BLK:KC], -jnp.inf),
                        ],
                        axis=0,
                    )
                new = jnp.maximum(top, jnp.max(fold(s, jnp.max), axis=0, keepdims=True) * LOG)
                e = jnp.exp2(s * LOG - new)
                s_buf[at[i], :] = e
                d_buf[at[i], :] = dp
                shrink = jnp.exp2(top - new)
                norm = norm * shrink + fold(e, jnp.sum)
                inner = inner * shrink + fold(e * dp, jnp.sum)
                top = new
                tops.append(new)
            inv = 1.0 / jnp.sum(norm, axis=0, keepdims=True)
            delta = jnp.sum(inner, axis=0, keepdims=True) * inv
            dq = jnp.zeros((DH, BLK), F32)
            for i in range(n):
                p = s_buf[at[i], :] * (jnp.exp2(tops[i] - top) * inv)
                ds = (p * (d_buf[at[i], :] - delta)).astype(BF16)
                soft = p.astype(BF16)
                for j in range(2):
                    p_buf[blk, 2 * i + j] = soft[j * BLK:(j + 1) * BLK]
                    ds_buf[blk, 2 * i + j] = ds[j * BLK:(j + 1) * BLK]
                dq = dq + jnp.dot(kt[i], ds, preferred_element_type=F32)
            dq_buf[rows, :] = dq.T * SCALE

        @pl.loop(0, blocks)
        def _(b):
            start = pl.multiple_of(b * BLK, BLK)
            pairs = lax.div(lax.div(start + BLK - 1, size), 2) + 2
            for n in range(3, NP + 1):
                pl.when(pairs == n)(functools.partial(rows_block, b, start, n))

    parts = (kall, vall)
    texts = (tk, tv)

    def wait_send(copy):
        copy.wait_send()

    def to_mate(i, j):
        s = 2 * j + 1 - core
        return push(parts[i].at[s], pair_in.at[i, j],
                    pair_send.at[i, j], pair_recv.at[i, j], mate)

    def text_to(i, t, slot):
        return push(texts[i], text_in.at[slot], text_send.at[i], text_recv.at[slot], t)

    def gq_out(t, size):
        return push(qall.at[t, pl.ds(0, size)], got_q.at[me, pl.ds(0, size)],
                    q_send.at[t], q_recv.at[me], t)

    def gq_self(size):
        return pltpu.make_async_copy(
            qall.at[me, pl.ds(0, size)], got_q.at[me, pl.ds(0, size)], q_local)

    def single_out(i, t):
        return push(parts[i].at[t], got.at[i, 2 * my_head + 1],
                    out_send.at[i, t], out_recv.at[i, 2 * my_head + 1], t)

    def pair_out(i, j):
        return push(pair_sum.at[i, j], got.at[i, 2 * my_head],
                    out_send.at[i, 2 * j + core], out_recv.at[i, 2 * my_head], 2 * j + core)

    def cast(t, n):
        return push(text_sum, text_all.at[my_head, core],
                    cast_send.at[n], cast_recv.at[my_head, core], t)

    def pass_on(h, t, sem):
        view = text_all.at[h, core]
        return push(view, view, sem, cast_recv.at[h, core], t)

    def await_text(h, kind):
        view = text_all.at[h, kind]
        await_recv(view, cast_send.at[0], cast_recv.at[h, kind], mate)

    def pair_text(act):
        pl.when(core == 0)(lambda: act(text_to(1, mate, 0)))
        pl.when(core == 1)(lambda: act(text_to(0, mate, 0)))

    def single_text(act):
        act(text_to(0, my_pair, 1))
        act(text_to(1, my_pair + 1, 1))

    def grads(chunk, last):
        gk = gv = 0
        for b in range(last):
            rows = slice(b * BLK, (b + 1) * BLK)
            gk = gk + jnp.dot(ds_buf[b, chunk], qs[rows, :], preferred_element_type=F32)
            gv = gv + jnp.dot(p_buf[b, chunk], gs[rows, :], preferred_element_type=F32)
        return gk * SCALE, gv

    def give(n):
        last = 6 if n == 96 else 5
        for r in range(NG):
            dq_rank[r, 0:n] = dq_buf[r * n:(r + 1) * n, :].astype(BF16)
        for s in range(NG):
            qall[s, 0:n] = dq_rank[group_of[s], 0:n]

        @pl.loop(1, NG)
        def _(d):
            gq_out(lax.rem(me + d, NG), n).start()

        gq_self(n).start()
        for i in range(2):
            gk, gv = grads(i, last)
            tk[i * BLK:(i + 1) * BLK, :] = gk.astype(BF16)
            tv[i * BLK:(i + 1) * BLK, :] = gv.astype(BF16)

        @pl.when(paired)
        def _():
            pair_text(start)

        pl.when(alone)(lambda: single_text(start))

        def half(parity, put):
            @pl.loop(0, 8)
            def _(n):
                j = lax.rem(lax.div(me, 2) + n, 8)
                t = 2 * j + parity
                put(j, t, grads(group_of[t] + 2, last))

        def keep(j, t, pair):
            for i in range(2):
                parts[i][t] = pair[i].astype(BF16)
            pl.when(paired)(lambda: [to_mate(i, j).start() for i in range(2)] and None)
            pl.when(alone & (t != me))(lambda: [single_out(i, t).start() for i in range(2)] and None)

            @pl.when(alone & (t == me))
            def _():
                for i in range(2):
                    got[i, 2 * my_head + 1] = pair[i].astype(BF16)

        def join(j, t, pair):
            for i in range(2):
                await_recv(pair_in.at[i, j], pair_send.at[i, j], pair_recv.at[i, j], mate)
                pair_sum[i, j] = (pair[i] + pair_in[i, j].astype(F32)).astype(BF16)

            @pl.when(t != me)
            def _():
                for i in range(2):
                    pair_out(i, j).start()

            @pl.when(t == me)
            def _():
                for i in range(2):
                    got[i, 2 * my_head] = pair_sum[i, j]

        half(1 - core, keep)

        @pl.when(paired)
        def _():
            for slot in range(2):
                await_recv(text_in.at[slot], text_send.at[0], text_recv.at[slot], mate)
            other = text_in[0].astype(F32) + text_in[1].astype(F32)

            @pl.when(core == 0)
            def _():
                text_sum[...] = (tk[...].astype(F32) + other).astype(BF16)

            @pl.when(core == 1)
            def _():
                text_sum[...] = (tv[...].astype(F32) + other).astype(BF16)

            cast(mirror, 0).start()
            for n in (1, 2, 3):
                cast(lax.rem(me + 4 * n, NG), n).start()
            text_all[my_head, core] = text_sum[...]
            half(core, join)

        pl.when(alone)(lambda: half(core, keep))

    pl.when(working)(lambda: by_third(my_part, give))

    for h in range(NH):
        source = 3 * h + h % 2 + core

        @pl.when(mirror == source)
        def _():
            await_text(h, core)
            for n in (1, 2, 3):
                pass_on(h, lax.rem(me + 4 * n, NG), relay_send.at[n]).start()

    for h in range(NH):
        source = 3 * h + h % 2 + core
        pl.when((mirror != source) & (me != source))(lambda: await_text(h, core))
        pass_on(h, mate, mate_send.at[h]).start()

    pl.when(working)(lambda: by_third(my_part, lambda size: gq_self(size).wait()))
    acc_q = jnp.zeros((BLK, DH), F32)
    acc_k = jnp.zeros((BLK, DH), F32)
    for h in range(NH):
        cols = slice(h * DH, (h + 1) * DH)
        pair = 3 * h + h % 2 + core
        single = 3 * h + 2 - 2 * (h % 2)
        for i in range(2):
            for slot, src in ((2 * h, pair), (2 * h + 1, single)):
                pl.when(src != me)(lambda: await_recv(
                    got.at[i, slot], out_send.at[i, 0], out_recv.at[i, slot], src))
        for p, at, size in ((0, 0, 96), (1, 96, 80), (2, 176, 80)):
            src = 3 * h + p
            pl.when(src != me)(lambda: await_recv(
                got_q.at[src, pl.ds(0, size)], q_send.at[0], q_recv.at[src], src))
            uq[at:at + size, cols] = got_q[src, 0:size].astype(F32) * gain_q[:, cols]
        u = (got[0, 2 * h].astype(F32) + got[0, 2 * h + 1].astype(F32)) * gain_k[:, cols]
        uk[:, cols] = u
        acc_k = acc_k + u * k_ref[:, cols].astype(F32)
        acc_q = acc_q + uq[:, cols] * q_ref[:, cols].astype(F32)
    copies = head_sum(row_sums(acc_q), row_sums(acc_k), sq_send.at[1], sq_recv.at[1], ss.at[1], rs.at[1], hd, nh)
    for h in range(NH):
        cols = slice(h * DH, (h + 1) * DH)
        dv[:, cols] = (got[1, 2 * h].astype(F32) + got[1, 2 * h + 1].astype(F32)).astype(BF16)
    for h in range(NH):
        cols = slice(h * DH, (h + 1) * DH)
        await_text(h, 1 - core)
        dtk[:, cols] = text_all[h, 0]
        dtv[:, cols] = text_all[h, 1]
    inner = head_total(copies, sq_send.at[1], sq_recv.at[1], nh) / (NH * DH * nh)
    cube = scale * scale * scale * inner
    for row, u_ref, x_ref, out in ((0, uq, q_ref, dq), (1, uk, k_ref, dk)):
        col = as_column(scale[row:row + 1])
        col3 = as_column(cube[row:row + 1])
        for h in range(NH):
            cols = slice(h * DH, (h + 1) * DH)
            out[:, cols] = (col * u_ref[:, cols] - x_ref[:, cols].astype(F32) * col3).astype(BF16)

    for h in range(NH):
        source = 3 * h + h % 2 + core
        pass_on(h, mate, mate_send.at[h]).wait_send()

        @pl.when(mirror == source)
        def _():
            for n in (1, 2, 3):
                pass_on(h, lax.rem(me + 4 * n, NG), relay_send.at[n]).wait_send()

    pl.when(alone)(lambda: single_text(wait_send))

    @pl.when(paired)
    def _():
        pair_text(wait_send)
        for n in range(4):
            cast(mate, n).wait_send()

        @pl.loop(0, 8)
        def _(j):
            for i in range(2):
                to_mate(i, j).wait_send()
                pl.when(2 * j + core != me)(lambda: pair_out(i, j).wait_send())

    @pl.when(working)
    def _():
        @pl.loop(1, NG)
        def _(d):
            t = lax.rem(me + d, NG)

            @pl.when(alone)
            def _():
                for i in range(2):
                    single_out(i, t).wait_send()

            by_third(my_part, lambda size: gq_out(t, size).wait_send())


def final_kernel(*refs):
    n = len(refs) // 2
    for src, dst in zip(refs[:n], refs[n:]):
        dst[...] = src[...]


VM = pl.BlockSpec(memory_space=pltpu.VMEM)
SM = pl.BlockSpec(memory_space=pltpu.SMEM)
ANY = pl.BlockSpec(memory_space=pl.ANY)
DMA = pltpu.SemaphoreType.DMA


def body(nh, queries, keys, values, text_keys, text_values, d_out, gain_q, gain_k, group_of):
    results = tuple(
        jax.ShapeDtypeStruct((n, NH * DH), BF16) for n in (BLK, BLK, BLK, 2 * BLK, 2 * BLK)
    )
    places = jnp.arange(NG, dtype=jnp.int32)
    order = jnp.sum(jnp.where(group_of[None, :] == places[:, None], places[None, :], 0), axis=1)
    grads = pl.pallas_call(
        functools.partial(attend_kernel, nh),
        out_shape=results,
        in_specs=[VM] * 4 + [ANY] * 2 + [VM] * 2 + [SM] * 2,
        out_specs=(VM,) * 5,
        scratch_shapes=[
            pltpu.VMEM((BLK, NH * DH), BF16),
            pltpu.VMEM((BLK, NH * DH), BF16),
            pltpu.VMEM((NG, BLK, DH), BF16),
            pltpu.VMEM((NG, BLK, DH), BF16),
            pltpu.VMEM((NG, 96, DH), BF16),
            pltpu.VMEM((NG, 96, DH), BF16),
            pltpu.VMEM((NP * KC, DH), BF16),
            pltpu.VMEM((NP * KC, DH), BF16),
            pltpu.VMEM((NP, DH, KC), BF16),
            pltpu.VMEM((ROWS, DH), BF16),
            pltpu.VMEM((ROWS, DH), BF16),
            pltpu.VMEM((NP * KC, BLK), F32),
            pltpu.VMEM((NP * KC, BLK), F32),
            pltpu.VMEM((6, 2 * NP, BLK, BLK), BF16),
            pltpu.VMEM((6, 2 * NP, BLK, BLK), BF16),
            pltpu.VMEM((ROWS, DH), F32),
            pltpu.VMEM((NG, 96, DH), BF16),
            pltpu.VMEM((KC, DH), BF16),
            pltpu.VMEM((KC, DH), BF16),
            pltpu.VMEM((2, 8, BLK, DH), BF16),
            pltpu.VMEM((2, 8, BLK, DH), BF16),
            pltpu.VMEM((2, 2 * NH, BLK, DH), BF16),
            pltpu.VMEM((NDEV, 96, DH), BF16),
            pltpu.VMEM((2, 2 * BLK, DH), BF16),
            pltpu.VMEM((2 * BLK, DH), BF16),
            pltpu.VMEM((NH, 2, 2 * BLK, DH), BF16),
            pltpu.VMEM((BLK, NH * DH), F32),
            pltpu.VMEM((BLK, NH * DH), F32),
            pltpu.VMEM((2, 8, BLK), F32),
            pltpu.VMEM((2, nh, 8, BLK), F32),
            DMA((4, NG)), DMA((4, NG)), DMA((4, NG)), DMA((4,)), DMA((2,)),
            DMA((2, 8)), DMA((2, 8)), DMA((2, NG)), DMA((2, 2 * NH)), DMA((NG,)), DMA((NG,)),
            DMA, DMA((2,)), DMA((2,)), DMA((4,)), DMA((NH, 2)), DMA((4,)), DMA((NH,)),
            DMA((2, nh)), DMA((2, nh)),
        ],
        compiler_params=pltpu.CompilerParams(
            collective_id=0, has_side_effects=True, vmem_limit_bytes=VMEM_LIMIT
        ),
        name="attend",
    )(queries, keys, values, d_out, text_keys, text_values, gain_q, gain_k, group_of, order)
    return pl.pallas_call(
        final_kernel,
        out_shape=results,
        in_specs=[VM] * 5,
        out_specs=(VM,) * 5,
        name="finish",
    )(*grads)


def solution(mesh):
    placed = (
        P("group", "head"),
        P("group", "head"),
        P("group", "head"),
        P(None, "head"),
        P(None, "head"),
        P("group", "head"),
        P("head"),
        P("head"),
        P(),
    )
    return jax.shard_map(
        functools.partial(body, mesh.shape["head"]),
        mesh=mesh,
        in_specs=placed,
        out_specs=(
            P("group", "head"),
            P("group", "head"),
            P("group", "head"),
            P(None, "head"),
            P(None, "head"),
        ),
        check_vma=False,
    )
```

```python
import functools
import math

import jax
import jax.numpy as jnp
from jax import lax
from jax.experimental import pallas as pl
from jax.experimental.pallas import tpu as pltpu
from jax.sharding import PartitionSpec as P

DH = 128
EPS = 1e-06
BLK = 256
NG = 16
NH = 5
HALF = 128
NB = 8
KC = 512
NP = 9
ROWS = 2048
SCALE = DH ** (-0.5)
LOG = SCALE * math.log2(math.e)
MESH = pl.DeviceIdType.MESH
F32 = jnp.float32
BF16 = jnp.bfloat16
VMEM_LIMIT = 62 * 1024 * 1024


def greet(me, hd, nh):
    barrier = pltpu.get_barrier_semaphore()
    for d in range(1, NG):
        pl.semaphore_signal(
            barrier, inc=1, device_id={"group": lax.rem(me + d, NG)}, device_id_type=MESH
        )
    for d in range(1, nh):
        pl.semaphore_signal(
            barrier, inc=1, device_id={"head": lax.rem(hd + d, nh)}, device_id_type=MESH
        )
    pl.semaphore_wait(barrier, NG - 1 + nh - 1)


def row_sums(acc):
    return jnp.sum(acc.T, axis=0, keepdims=True)


def as_column(row):
    return jnp.broadcast_to(row, (DH, BLK)).T


def head_sum(row_q, row_k, send, recv, send_sem, recv_sem, hd, nh):
    send[...] = jnp.concatenate([row_q, row_k, jnp.zeros((6, BLK), F32)], axis=0)
    copies = []
    for d in range(1, nh):
        peer = lax.rem(hd + d, nh)
        copy = pltpu.make_async_remote_copy(
            src_ref=send,
            dst_ref=recv.at[d],
            send_sem=send_sem.at[d],
            recv_sem=recv_sem.at[d],
            device_id={"head": peer},
            device_id_type=MESH,
        )
        copy.start()
        copies.append(copy)
    return copies


def head_total(copies, send, recv, nh):
    for copy in copies:
        copy.wait()
    total = send[...]
    for d in range(1, nh):
        total = total + recv[d]
    return total


def base_of(h):
    return 2 * (h + 2 * (h // 3))


def push(src, dst, send_sem, recv_sem, t):
    return pltpu.make_async_remote_copy(
        src_ref=src, dst_ref=dst, send_sem=send_sem, recv_sem=recv_sem,
        device_id={"group": t}, device_id_type=MESH,
    )


def await_recv(dst, send_sem, recv_sem, t):
    push(dst, dst, send_sem, recv_sem, t).wait_recv()


def head_cols(h):
    return pl.ds(pl.multiple_of(h * DH, DH), DH)


def attend_kernel(
    nh, q_ref, k_ref, v_ref, g_ref, tk_ref, tv_ref, gain_q_ref, gain_k_ref, group_of, order,
    dq, dk, dv, dtk, dtv,
    qn, kn, kall, vall, qall, gall, ks, vs, kt, qs, gs, s_buf, d_buf, p_bufs, ds_bufs, dq_buf, dq_rank,
    tk, tv, pair_in, pair_sum, got, got_q, text_in, text_sum, text_all, uq, uk, sq_send, sq_recv,
    in_send, in_recv, relay_sem, local_sem, text_sem,
    pair_send, pair_recv, out_send, out_recv, q_send, q_recv, q_local,
    text_send, text_recv, cast_send, cast_recv, relay_send, mate_send, ss, rs,
):
    me = lax.axis_index("group")
    hd = lax.axis_index("head")
    core = lax.rem(me, 2)
    mate = me + 1 - 2 * core
    mirror = me + 2 - 4 * lax.rem(lax.div(me, 2), 2)
    chip = lax.div(me, 2)
    my_head = chip - 2 * lax.div(chip, 5)
    working = (chip < 3) | (chip == 5) | (chip == 6)
    gain_q = gain_q_ref[...].astype(F32)[None, :]
    gain_k = gain_k_ref[...].astype(F32)[None, :]

    def text_copy(i):
        return pltpu.make_async_copy(
            (tk_ref, tv_ref)[i].at[:, head_cols(my_head)], (ks, vs)[i].at[pl.ds(0, KC)],
            text_sem.at[i])

    pl.when(working)(lambda: [text_copy(i).start() for i in range(2)] and None)
    greet(me, hd, nh)

    whole = ((0, v_ref, vall), (2, kn, kall))
    halves = ((1, g_ref, gall), (3, qn, qall))

    def half_src(ref, h, part):
        return ref.at[pl.ds(pl.multiple_of(part * HALF, HALF), HALF), head_cols(h)]

    def to_all(stage, act):
        kind, ref, out = whole[stage]
        kind2, ref2, out2 = halves[stage]

        @pl.loop(0, NH)
        def _(d):
            h = lax.rem(my_head + 1 + d, NH)
            base = 2 * (h + 2 * lax.div(h, 3))

            @pl.when(base + core != me)
            def _():
                act(push(ref.at[:, head_cols(h)], out.at[me],
                         in_send.at[kind, 2 * h + core], in_recv.at[kind, me], base + core))

            for part in range(2):
                @pl.when(base + part != me)
                def _():
                    act(push(half_src(ref2, h, part), out2.at[me],
                             in_send.at[kind2, 2 * h + part], in_recv.at[kind2, me], base + part))

    def to_self(stage, act):
        kind, ref, out = whole[stage]
        kind2, ref2, out2 = halves[stage]

        @pl.when(working)
        def _():
            act(pltpu.make_async_copy(
                ref.at[:, head_cols(my_head)], out.at[me], local_sem.at[kind]))
            act(pltpu.make_async_copy(
                half_src(ref2, my_head, core), out2.at[me], local_sem.at[kind2]))

    def start(copy):
        copy.start()

    def relay(stage, s):
        kind, ref, out = whole[stage]
        view = out.at[s]
        return push(view, view, relay_sem.at[kind, s], in_recv.at[kind, s], mate)

    def relay_all(stage):
        kind, ref, out = whole[stage]

        @pl.when(working)
        def _():
            relay(stage, me).start()

            @pl.loop(1, 8)
            def _(d):
                s = lax.rem(me + NG - 2 * d, NG)
                await_recv(out.at[s], in_send.at[kind, 0], in_recv.at[kind, s], s)
                relay(stage, s).start()

    acc_q = jnp.zeros((BLK, DH), F32)
    acc_k = jnp.zeros((BLK, DH), F32)
    for h in range(NH):
        cols = slice(h * DH, (h + 1) * DH)
        x = q_ref[:, cols].astype(F32)
        acc_q = acc_q + x * x
        x = k_ref[:, cols].astype(F32)
        acc_k = acc_k + x * x
    copies = head_sum(row_sums(acc_q), row_sums(acc_k), sq_send.at[0], sq_recv.at[0], ss.at[0], rs.at[0], hd, nh)
    to_all(0, start)
    to_self(0, start)
    total = head_total(copies, sq_send.at[0], sq_recv.at[0], nh)
    scale = lax.rsqrt(total / (NH * DH * nh) + EPS)
    col_q = as_column(scale[0:1])
    col_k = as_column(scale[1:2])
    for h in range(NH):
        cols = slice(h * DH, (h + 1) * DH)
        kn[:, cols] = (k_ref[:, cols].astype(F32) * col_k * gain_k[:, cols]).astype(BF16)
        qn[:, cols] = (q_ref[:, cols].astype(F32) * col_q * gain_q[:, cols]).astype(BF16)
    to_all(1, start)
    to_self(1, start)

    to_self(0, lambda copy: copy.wait())
    relay_all(0)
    to_self(1, lambda copy: copy.wait())
    relay_all(1)

    @pl.when(working)
    def _():
        @pl.loop(1, NG)
        def _(d):
            s = lax.rem(me + d, NG)

            @pl.when(lax.rem(d, 2) == 1)
            def _():
                for kind, ref, out in whole:
                    await_recv(out.at[s], in_send.at[kind, 0], in_recv.at[kind, s], s)

            for kind, ref, out in halves:
                await_recv(out.at[s], in_send.at[kind, 0], in_recv.at[kind, s], s)

    @pl.when(working)
    def _():
        @pl.loop(0, 8)
        def _(d):
            s = lax.rem(me + 2 * d, NG)
            for stage in range(2):
                relay(stage, s).wait_send()

    for stage in range(2):
        to_all(stage, lambda copy: copy.wait_send())

    @pl.when(working)
    def _():
        for i in range(2):
            text_copy(i).wait()

        for r in range(NG):
            qs[r * HALF:(r + 1) * HALF, :] = qall[order[r]]
            gs[r * HALF:(r + 1) * HALF, :] = gall[order[r]]
        for r in range(NG):
            ks[(r + 2) * BLK:(r + 3) * BLK, :] = kall[order[r]]
            vs[(r + 2) * BLK:(r + 3) * BLK, :] = vall[order[r]]
        for i in range(NP):
            kt[i] = ks[i * KC:(i + 1) * KC, :].T

        def fold(x, op):
            return op(x.reshape(x.shape[0] // 8, 8, x.shape[-1]), axis=0)

        def rows_block(b):
            n = b + 2
            rows = slice(b * BLK, (b + 1) * BLK)
            q_cols = qs[rows, :].T
            g_cols = gs[rows, :].T
            later = lax.broadcasted_iota(jnp.int32, (1, BLK), 1) >= HALF
            at = [slice(i * KC, (i + 1) * KC) for i in range(n)]
            top = jnp.full((1, BLK), -jnp.inf, F32)
            norm = jnp.zeros((8, BLK), F32)
            inner = jnp.zeros((8, BLK), F32)
            tops = []
            for i in range(n):
                s = jnp.dot(ks[at[i], :], q_cols, preferred_element_type=F32)
                dp = jnp.dot(vs[at[i], :], g_cols, preferred_element_type=F32)
                if i == n - 1:
                    s = jnp.concatenate([s[0:BLK], jnp.where(later, s[BLK:KC], -jnp.inf)], axis=0)
                new = jnp.maximum(top, jnp.max(fold(s, jnp.max), axis=0, keepdims=True) * LOG)
                e = jnp.exp2(s * LOG - new)
                s_buf[at[i], :] = e
                d_buf[at[i], :] = dp
                shrink = jnp.exp2(top - new)
                norm = norm * shrink + fold(e, jnp.sum)
                inner = inner * shrink + fold(e * dp, jnp.sum)
                top = new
                tops.append(new)
            inv = 1.0 / jnp.sum(norm, axis=0, keepdims=True)
            delta = jnp.sum(inner, axis=0, keepdims=True) * inv
            dq = jnp.zeros((DH, BLK), F32)
            for i in range(n):
                p = s_buf[at[i], :] * (jnp.exp2(tops[i] - top) * inv)
                ds = (p * (d_buf[at[i], :] - delta)).astype(BF16)
                soft = p.astype(BF16)
                for j in range(2):
                    p_bufs[b][2 * i + j] = soft[j * BLK:(j + 1) * BLK]
                    ds_bufs[b][2 * i + j] = ds[j * BLK:(j + 1) * BLK]
                dq = dq + jnp.dot(kt[i], ds, preferred_element_type=F32)
            dq_buf[rows, :] = dq.T * SCALE

        for b in range(NB):
            rows_block(b)

    parts = (kall, vall)
    texts = (tk, tv)

    def wait_send(copy):
        copy.wait_send()

    def to_mate(i, j):
        return push(parts[i].at[2 * j + 1 - core], pair_in.at[i, j],
                    pair_send.at[i, j], pair_recv.at[i, j], mate)

    def text_to(i):
        return push(texts[i], text_in, text_send, text_recv, mate)

    def gq_out(t):
        return push(qall.at[t], got_q.at[2 * my_head + core],
                    q_send.at[t], q_recv.at[2 * my_head + core], t)

    def gq_self():
        return pltpu.make_async_copy(qall.at[me], got_q.at[2 * my_head + core], q_local)

    def pair_out(i, j):
        return push(pair_sum.at[i, j], got.at[i, my_head],
                    out_send.at[i, j], out_recv.at[i, my_head], 2 * j + core)

    def cast(t, n):
        return push(text_sum, text_all.at[my_head, core],
                    cast_send.at[n], cast_recv.at[my_head, core], t)

    def pass_on(h, t, sem):
        view = text_all.at[h, core]
        return push(view, view, sem, cast_recv.at[h, core], t)

    def await_text(h, kind):
        view = text_all.at[h, kind]
        await_recv(view, cast_send.at[0], cast_recv.at[h, kind], mate)

    def pair_text(act):
        pl.when(core == 0)(lambda: act(text_to(1)))
        pl.when(core == 1)(lambda: act(text_to(0)))

    def grads(chunk):
        gk = gv = 0
        for b in range(NB):
            rows = slice(b * BLK, (b + 1) * BLK)
            last = 2 * b + 3
            index = jnp.minimum(chunk, last)
            here_k = jnp.dot(ds_bufs[b][index], qs[rows, :], preferred_element_type=F32)
            here_v = jnp.dot(p_bufs[b][index], gs[rows, :], preferred_element_type=F32)
            if b < NB - 1:
                seen = (chunk <= last).astype(F32)
                here_k, here_v = here_k * seen, here_v * seen
            gk, gv = gk + here_k, gv + here_v
        return gk * SCALE, gv

    @pl.when(working)
    def _():
        for r in range(NG):
            dq_rank[r] = dq_buf[r * HALF:(r + 1) * HALF, :].astype(BF16)
        for s in range(NG):
            qall[s] = dq_rank[group_of[s]]

        @pl.loop(1, NG)
        def _(d):
            gq_out(lax.rem(me + d, NG)).start()

        gq_self().start()

        @pl.loop(0, 2)
        def _(i):
            gk, gv = grads(i)
            place = pl.ds(pl.multiple_of(i * BLK, BLK), BLK)
            tk[place, :] = gk.astype(BF16)
            tv[place, :] = gv.astype(BF16)

        pair_text(start)

        def each(put):
            @pl.loop(0, 8)
            def _(n):
                put(lax.rem(chip + n, 8))

        def keep(j):
            t = 2 * j + 1 - core
            pair = grads(group_of[t] + 2)
            for i in range(2):
                parts[i][t] = pair[i].astype(BF16)
                to_mate(i, j).start()

        def join(j):
            t = 2 * j + core
            pair = grads(group_of[t] + 2)
            for i in range(2):
                await_recv(pair_in.at[i, j], pair_send.at[i, j], pair_recv.at[i, j], mate)
                pair_sum[i, j] = (pair[i] + pair_in[i, j].astype(F32)).astype(BF16)
                pl.when(t != me)(lambda: pair_out(i, j).start())

                @pl.when(t == me)
                def _():
                    got[i, my_head] = pair_sum[i, j]

        each(keep)
        await_recv(text_in, text_send, text_recv, mate)

        @pl.when(core == 0)
        def _():
            text_sum[...] = (tk[...].astype(F32) + text_in[...].astype(F32)).astype(BF16)

        @pl.when(core == 1)
        def _():
            text_sum[...] = (tv[...].astype(F32) + text_in[...].astype(F32)).astype(BF16)

        cast(mirror, 0).start()
        for n in (1, 2, 3):
            cast(lax.rem(me + 4 * n, NG), n).start()
        text_all[my_head, core] = text_sum[...]
        each(join)

    for h in range(NH):
        source = base_of(h) + core

        @pl.when(mirror == source)
        def _():
            await_text(h, core)
            for n in (1, 2, 3):
                pass_on(h, lax.rem(me + 4 * n, NG), relay_send.at[n]).start()

    for h in range(NH):
        source = base_of(h) + core
        pl.when((mirror != source) & (me != source))(lambda: await_text(h, core))
        pass_on(h, mate, mate_send.at[h]).start()

    pl.when(working)(lambda: gq_self().wait())
    acc_q = jnp.zeros((BLK, DH), F32)
    acc_k = jnp.zeros((BLK, DH), F32)
    for h in range(NH):
        cols = slice(h * DH, (h + 1) * DH)
        for i in range(2):
            pl.when(base_of(h) + core != me)(lambda: await_recv(
                got.at[i, h], out_send.at[i, 0], out_recv.at[i, h], base_of(h) + core))
        for p in range(2):
            pl.when(base_of(h) + p != me)(lambda: await_recv(
                got_q.at[2 * h + p], q_send.at[0], q_recv.at[2 * h + p], base_of(h) + p))
            uq[p * HALF:(p + 1) * HALF, cols] = got_q[2 * h + p].astype(F32) * gain_q[:, cols]
        u = got[0, h].astype(F32) * gain_k[:, cols]
        uk[:, cols] = u
        acc_k = acc_k + u * k_ref[:, cols].astype(F32)
        acc_q = acc_q + uq[:, cols] * q_ref[:, cols].astype(F32)
    copies = head_sum(row_sums(acc_q), row_sums(acc_k), sq_send.at[1], sq_recv.at[1], ss.at[1], rs.at[1], hd, nh)
    for h in range(NH):
        cols = slice(h * DH, (h + 1) * DH)
        dv[:, cols] = got[1, h]
    for h in range(NH):
        cols = slice(h * DH, (h + 1) * DH)
        await_text(h, 1 - core)
        dtk[:, cols] = text_all[h, 0]
        dtv[:, cols] = text_all[h, 1]
    inner = head_total(copies, sq_send.at[1], sq_recv.at[1], nh) / (NH * DH * nh)
    cube = scale * scale * scale * inner
    for row, u_ref, x_ref, out in ((0, uq, q_ref, dq), (1, uk, k_ref, dk)):
        col = as_column(scale[row:row + 1])
        col3 = as_column(cube[row:row + 1])
        for h in range(NH):
            cols = slice(h * DH, (h + 1) * DH)
            out[:, cols] = (col * u_ref[:, cols] - x_ref[:, cols].astype(F32) * col3).astype(BF16)

    for h in range(NH):
        source = base_of(h) + core
        pass_on(h, mate, mate_send.at[h]).wait_send()

        @pl.when(mirror == source)
        def _():
            for n in (1, 2, 3):
                pass_on(h, lax.rem(me + 4 * n, NG), relay_send.at[n]).wait_send()

    @pl.when(working)
    def _():
        pair_text(wait_send)
        for n in range(4):
            cast(mate, n).wait_send()

        @pl.loop(0, 8)
        def _(j):
            for i in range(2):
                to_mate(i, j).wait_send()
                pl.when(2 * j + core != me)(lambda: pair_out(i, j).wait_send())

        @pl.loop(1, NG)
        def _(d):
            gq_out(lax.rem(me + d, NG)).wait_send()


def final_kernel(*refs):
    n = len(refs) // 2
    for src, dst in zip(refs[:n], refs[n:]):
        dst[...] = src[...]


VM = pl.BlockSpec(memory_space=pltpu.VMEM)
SM = pl.BlockSpec(memory_space=pltpu.SMEM)
ANY = pl.BlockSpec(memory_space=pl.ANY)
DMA = pltpu.SemaphoreType.DMA


def body(nh, queries, keys, values, text_keys, text_values, d_out, gain_q, gain_k, group_of):
    results = tuple(
        jax.ShapeDtypeStruct((n, NH * DH), BF16) for n in (BLK, BLK, BLK, 2 * BLK, 2 * BLK)
    )
    places = jnp.arange(NG, dtype=jnp.int32)
    order = jnp.sum(jnp.where(group_of[None, :] == places[:, None], places[None, :], 0), axis=1)
    grads = pl.pallas_call(
        functools.partial(attend_kernel, nh),
        out_shape=results,
        in_specs=[VM] * 4 + [ANY] * 2 + [VM] * 2 + [SM] * 2,
        out_specs=(VM,) * 5,
        scratch_shapes=[
            pltpu.VMEM((BLK, NH * DH), BF16),
            pltpu.VMEM((BLK, NH * DH), BF16),
            pltpu.VMEM((NG, BLK, DH), BF16),
            pltpu.VMEM((NG, BLK, DH), BF16),
            pltpu.VMEM((NG, HALF, DH), BF16),
            pltpu.VMEM((NG, HALF, DH), BF16),
            pltpu.VMEM((NP * KC, DH), BF16),
            pltpu.VMEM((NP * KC, DH), BF16),
            pltpu.VMEM((NP, DH, KC), BF16),
            pltpu.VMEM((ROWS, DH), BF16),
            pltpu.VMEM((ROWS, DH), BF16),
            pltpu.VMEM((NP * KC, BLK), F32),
            pltpu.VMEM((NP * KC, BLK), F32),
            [pltpu.VMEM((2 * b + 4, BLK, BLK), BF16) for b in range(NB)],
            [pltpu.VMEM((2 * b + 4, BLK, BLK), BF16) for b in range(NB)],
            pltpu.VMEM((ROWS, DH), F32),
            pltpu.VMEM((NG, HALF, DH), BF16),
            pltpu.VMEM((KC, DH), BF16),
            pltpu.VMEM((KC, DH), BF16),
            pltpu.VMEM((2, 8, BLK, DH), BF16),
            pltpu.VMEM((2, 8, BLK, DH), BF16),
            pltpu.VMEM((2, NH, BLK, DH), BF16),
            pltpu.VMEM((2 * NH, HALF, DH), BF16),
            pltpu.VMEM((2 * BLK, DH), BF16),
            pltpu.VMEM((2 * BLK, DH), BF16),
            pltpu.VMEM((NH, 2, 2 * BLK, DH), BF16),
            pltpu.VMEM((BLK, NH * DH), F32),
            pltpu.VMEM((BLK, NH * DH), F32),
            pltpu.VMEM((2, 8, BLK), F32),
            pltpu.VMEM((2, nh, 8, BLK), F32),
            DMA((4, NG)), DMA((4, NG)), DMA((4, NG)), DMA((4,)), DMA((2,)),
            DMA((2, 8)), DMA((2, 8)), DMA((2, 8)), DMA((2, NH)), DMA((NG,)), DMA((2 * NH,)),
            DMA, DMA, DMA, DMA((4,)), DMA((NH, 2)), DMA((4,)), DMA((NH,)),
            DMA((2, nh)), DMA((2, nh)),
        ],
        compiler_params=pltpu.CompilerParams(
            collective_id=0, has_side_effects=True, vmem_limit_bytes=VMEM_LIMIT
        ),
        name="attend",
    )(queries, keys, values, d_out, text_keys, text_values, gain_q, gain_k, group_of, order)
    return pl.pallas_call(
        final_kernel,
        out_shape=results,
        in_specs=[VM] * 5,
        out_specs=(VM,) * 5,
        name="finish",
    )(*grads)


def solution(mesh):
    placed = (
        P("group", "head"),
        P("group", "head"),
        P("group", "head"),
        P(None, "head"),
        P(None, "head"),
        P("group", "head"),
        P("head"),
        P("head"),
        P(),
    )
    return jax.shard_map(
        functools.partial(body, mesh.shape["head"]),
        mesh=mesh,
        in_specs=placed,
        out_specs=(
            P("group", "head"),
            P("group", "head"),
            P("group", "head"),
            P(None, "head"),
            P(None, "head"),
        ),
        check_vma=False,
    )
```

```python
import functools
import math

import jax
import jax.numpy as jnp
from jax import lax
from jax.experimental import pallas as pl
from jax.experimental.pallas import tpu as pltpu
from jax.sharding import PartitionSpec as P

DH = 128
EPS = 1e-06
BLK = 256
NG = 16
NH = 5
HALF = 128
NB = 8
KC = 512
NP = 9
ROWS = 2048
SCALE = DH ** (-0.5)
LOG = SCALE * math.log2(math.e)
MESH = pl.DeviceIdType.MESH
F32 = jnp.float32
BF16 = jnp.bfloat16
VMEM_LIMIT = 62 * 1024 * 1024


def greet(me, hd, nh):
    barrier = pltpu.get_barrier_semaphore()
    for d in range(1, NG):
        pl.semaphore_signal(
            barrier, inc=1, device_id={"group": lax.rem(me + d, NG)}, device_id_type=MESH
        )
    for d in range(1, nh):
        pl.semaphore_signal(
            barrier, inc=1, device_id={"head": lax.rem(hd + d, nh)}, device_id_type=MESH
        )
    return lambda: pl.semaphore_wait(barrier, NG - 1 + nh - 1)


def row_sums(acc):
    return jnp.sum(acc.T, axis=0, keepdims=True)


def as_column(row):
    return jnp.broadcast_to(row, (DH, BLK)).T


def head_sum(row_q, row_k, send, recv, send_sem, recv_sem, hd, nh):
    send[...] = jnp.concatenate([row_q, row_k, jnp.zeros((6, BLK), F32)], axis=0)
    copies = []
    for d in range(1, nh):
        peer = lax.rem(hd + d, nh)
        copy = pltpu.make_async_remote_copy(
            src_ref=send,
            dst_ref=recv.at[d],
            send_sem=send_sem.at[d],
            recv_sem=recv_sem.at[d],
            device_id={"head": peer},
            device_id_type=MESH,
        )
        copy.start()
        copies.append(copy)
    return copies


def head_total(copies, send, recv, nh):
    for copy in copies:
        copy.wait()
    total = send[...]
    for d in range(1, nh):
        total = total + recv[d]
    return total


def base_of(h):
    return 2 * (h + 2 * (h // 3))


def push(src, dst, send_sem, recv_sem, t):
    return pltpu.make_async_remote_copy(
        src_ref=src, dst_ref=dst, send_sem=send_sem, recv_sem=recv_sem,
        device_id={"group": t}, device_id_type=MESH,
    )


def await_recv(dst, send_sem, recv_sem, t):
    push(dst, dst, send_sem, recv_sem, t).wait_recv()


def head_cols(h):
    return pl.ds(pl.multiple_of(h * DH, DH), DH)


def attend_kernel(
    nh, q_ref, k_ref, v_ref, g_ref, tk_ref, tv_ref, gain_q_ref, gain_k_ref, group_of,
    dq, dk, dv, dtk, dtv,
    qn, kn, kall, vall, qall, gall, ks, vs, kt, qs, gs, s_buf, d_buf, p_bufs, ds_bufs, dq_buf, dq_rank,
    tk, tv, pair_in, pair_sum, got, got_q, text_in, text_sum, text_all, uq, uk, sq_send, sq_recv,
    in_send, in_recv, relay_sem, local_sem, text_sem,
    pair_send, pair_recv, out_send, out_recv, q_send, q_recv, q_local,
    text_send, text_recv, cast_send, cast_recv, relay_send, mate_send, ss, rs,
):
    me = lax.axis_index("group")
    hd = lax.axis_index("head")
    core = lax.rem(me, 2)
    mate = me + 1 - 2 * core
    mirror = me + 2 - 4 * lax.rem(lax.div(me, 2), 2)
    chip = lax.div(me, 2)
    my_head = chip - 2 * lax.div(chip, 5)
    working = (chip < 3) | (chip == 5) | (chip == 6)
    gain_q = gain_q_ref[...].astype(F32)[None, :]
    gain_k = gain_k_ref[...].astype(F32)[None, :]

    def text_copy(i):
        return pltpu.make_async_copy(
            (tk_ref, tv_ref)[i].at[:, head_cols(my_head)], (ks, vs)[i].at[pl.ds(0, KC)],
            text_sem.at[i])

    pl.when(working)(lambda: [text_copy(i).start() for i in range(2)] and None)
    met = greet(me, hd, nh)

    whole = ((0, v_ref, vall), (2, kn, kall))
    halves = ((1, g_ref, gall), (3, qn, qall))

    def half_src(ref, h, part):
        return ref.at[pl.ds(pl.multiple_of(part * HALF, HALF), HALF), head_cols(h)]

    def to_all(stage, act):
        kind, ref, out = whole[stage]
        kind2, ref2, out2 = halves[stage]

        @pl.loop(0, NH)
        def _(d):
            h = lax.rem(my_head + 1 + d, NH)
            base = 2 * (h + 2 * lax.div(h, 3))

            @pl.when(base + core != me)
            def _():
                act(push(ref.at[:, head_cols(h)], out.at[me],
                         in_send.at[kind, 2 * h + core], in_recv.at[kind, me], base + core))

            for part in range(2):
                @pl.when(base + part != me)
                def _():
                    act(push(half_src(ref2, h, part), out2.at[me],
                             in_send.at[kind2, 2 * h + part], in_recv.at[kind2, me], base + part))

    def to_self(stage, act):
        kind, ref, out = whole[stage]
        kind2, ref2, out2 = halves[stage]

        @pl.when(working)
        def _():
            act(pltpu.make_async_copy(
                ref.at[:, head_cols(my_head)], out.at[me], local_sem.at[kind]))
            act(pltpu.make_async_copy(
                half_src(ref2, my_head, core), out2.at[me], local_sem.at[kind2]))

    def start(copy):
        copy.start()

    def relay(stage, s):
        kind, ref, out = whole[stage]
        view = out.at[s]
        return push(view, view, relay_sem.at[kind, s], in_recv.at[kind, s], mate)

    def relay_all(stage):
        kind, ref, out = whole[stage]

        @pl.when(working)
        def _():
            relay(stage, me).start()

            @pl.loop(1, 8)
            def _(d):
                s = lax.rem(me + NG - 2 * d, NG)
                await_recv(out.at[s], in_send.at[kind, 0], in_recv.at[kind, s], s)
                relay(stage, s).start()

    acc_q = jnp.zeros((BLK, DH), F32)
    acc_k = jnp.zeros((BLK, DH), F32)
    for h in range(NH):
        cols = slice(h * DH, (h + 1) * DH)
        x = q_ref[:, cols].astype(F32)
        acc_q = acc_q + x * x
        x = k_ref[:, cols].astype(F32)
        acc_k = acc_k + x * x
    sums = row_sums(acc_q), row_sums(acc_k)
    order = [
        jnp.minimum(
            sum((group_of[t] == r).astype(jnp.int32) * t for t in range(1, NG)), NG - 1)
        for r in range(NG)
    ]
    met()
    copies = head_sum(*sums, sq_send.at[0], sq_recv.at[0], ss.at[0], rs.at[0], hd, nh)
    to_all(0, start)
    to_self(0, start)
    total = head_total(copies, sq_send.at[0], sq_recv.at[0], nh)
    scale = lax.rsqrt(total / (NH * DH * nh) + EPS)
    col_q = as_column(scale[0:1])
    col_k = as_column(scale[1:2])
    for h in range(NH):
        cols = slice(h * DH, (h + 1) * DH)
        kn[:, cols] = (k_ref[:, cols].astype(F32) * col_k * gain_k[:, cols]).astype(BF16)
        qn[:, cols] = (q_ref[:, cols].astype(F32) * col_q * gain_q[:, cols]).astype(BF16)
    to_all(1, start)
    to_self(1, start)

    to_self(0, lambda copy: copy.wait())
    relay_all(0)
    to_self(1, lambda copy: copy.wait())
    relay_all(1)

    @pl.when(working)
    def _():
        @pl.loop(1, NG)
        def _(d):
            s = lax.rem(me + d, NG)

            @pl.when(lax.rem(d, 2) == 1)
            def _():
                for kind, ref, out in whole:
                    await_recv(out.at[s], in_send.at[kind, 0], in_recv.at[kind, s], s)

            for kind, ref, out in halves:
                await_recv(out.at[s], in_send.at[kind, 0], in_recv.at[kind, s], s)

    @pl.when(working)
    def _():
        @pl.loop(0, 8)
        def _(d):
            s = lax.rem(me + 2 * d, NG)
            for stage in range(2):
                relay(stage, s).wait_send()

    for stage in range(2):
        to_all(stage, lambda copy: copy.wait_send())

    @pl.when(working)
    def _():
        for i in range(2):
            text_copy(i).wait()

        for r in range(NG):
            qs[r * HALF:(r + 1) * HALF, :] = qall[order[r]]
            gs[r * HALF:(r + 1) * HALF, :] = gall[order[r]]
        for r in range(NG):
            ks[(r + 2) * BLK:(r + 3) * BLK, :] = kall[order[r]]
            vs[(r + 2) * BLK:(r + 3) * BLK, :] = vall[order[r]]
        for i in range(NP):
            kt[i] = ks[i * KC:(i + 1) * KC, :].T

        def fold(x, op):
            return op(x.reshape(x.shape[0] // 8, 8, x.shape[-1]), axis=0)

        def rows_block(b):
            n = b + 2
            rows = slice(b * BLK, (b + 1) * BLK)
            q_cols = qs[rows, :].T
            g_cols = gs[rows, :].T
            later = lax.broadcasted_iota(jnp.int32, (1, BLK), 1) >= HALF
            at = [slice(i * KC, (i + 1) * KC) for i in range(n)]
            top = jnp.full((1, BLK), -jnp.inf, F32)
            norm = jnp.zeros((8, BLK), F32)
            inner = jnp.zeros((8, BLK), F32)
            tops = []
            for i in range(n):
                s = jnp.dot(ks[at[i], :], q_cols, preferred_element_type=F32)
                dp = jnp.dot(vs[at[i], :], g_cols, preferred_element_type=F32)
                if i == n - 1:
                    s = jnp.concatenate([s[0:BLK], jnp.where(later, s[BLK:KC], -jnp.inf)], axis=0)
                new = jnp.maximum(top, jnp.max(fold(s, jnp.max), axis=0, keepdims=True) * LOG)
                e = jnp.exp2(s * LOG - new)
                s_buf[at[i], :] = e
                d_buf[at[i], :] = dp
                shrink = jnp.exp2(top - new)
                norm = norm * shrink + fold(e, jnp.sum)
                inner = inner * shrink + fold(e * dp, jnp.sum)
                top = new
                tops.append(new)
            inv = 1.0 / jnp.sum(norm, axis=0, keepdims=True)
            delta = jnp.sum(inner, axis=0, keepdims=True) * inv
            dq = jnp.zeros((DH, BLK), F32)
            for i in range(n):
                p = s_buf[at[i], :] * (jnp.exp2(tops[i] - top) * inv)
                ds = (p * (d_buf[at[i], :] - delta)).astype(BF16)
                soft = p.astype(BF16)
                for j in range(2):
                    p_bufs[b][2 * i + j] = soft[j * BLK:(j + 1) * BLK]
                    ds_bufs[b][2 * i + j] = ds[j * BLK:(j + 1) * BLK]
                dq = dq + jnp.dot(kt[i], ds, preferred_element_type=F32)
            dq_buf[rows, :] = dq.T * SCALE

        for b in range(NB):
            rows_block(b)

    parts = (kall, vall)
    texts = (tk, tv)

    def wait_send(copy):
        copy.wait_send()

    def to_mate(i, j):
        return push(parts[i].at[2 * j + 1 - core], pair_in.at[i, j],
                    pair_send.at[i, j], pair_recv.at[i, j], mate)

    def text_to(i):
        return push(texts[i], text_in, text_send, text_recv, mate)

    def gq_out(t):
        return push(qall.at[t], got_q.at[2 * my_head + core],
                    q_send.at[t], q_recv.at[2 * my_head + core], t)

    def gq_self():
        return pltpu.make_async_copy(qall.at[me], got_q.at[2 * my_head + core], q_local)

    def pair_out(i, j):
        return push(pair_sum.at[i, j], got.at[i, my_head],
                    out_send.at[i, j], out_recv.at[i, my_head], 2 * j + core)

    def cast(t, n):
        return push(text_sum, text_all.at[my_head, core],
                    cast_send.at[n], cast_recv.at[my_head, core], t)

    def pass_on(h, t, sem):
        view = text_all.at[h, core]
        return push(view, view, sem, cast_recv.at[h, core], t)

    def await_text(h, kind):
        view = text_all.at[h, kind]
        await_recv(view, cast_send.at[0], cast_recv.at[h, kind], mate)

    def pair_text(act):
        pl.when(core == 0)(lambda: act(text_to(1)))
        pl.when(core == 1)(lambda: act(text_to(0)))

    def grads(chunk):
        gk = gv = 0
        for b in range(NB):
            rows = slice(b * BLK, (b + 1) * BLK)
            last = 2 * b + 3
            index = jnp.minimum(chunk, last)
            here_k = jnp.dot(ds_bufs[b][index], qs[rows, :], preferred_element_type=F32)
            here_v = jnp.dot(p_bufs[b][index], gs[rows, :], preferred_element_type=F32)
            if b < NB - 1:
                seen = (chunk <= last).astype(F32)
                here_k, here_v = here_k * seen, here_v * seen
            gk, gv = gk + here_k, gv + here_v
        return gk * SCALE, gv

    @pl.when(working)
    def _():
        for r in range(NG):
            dq_rank[r] = dq_buf[r * HALF:(r + 1) * HALF, :].astype(BF16)
        for s in range(NG):
            qall[s] = dq_rank[group_of[s]]

        @pl.loop(1, NG)
        def _(d):
            gq_out(lax.rem(me + d, NG)).start()

        gq_self().start()

        @pl.loop(0, 2)
        def _(i):
            gk, gv = grads(i)
            place = pl.ds(pl.multiple_of(i * BLK, BLK), BLK)
            tk[place, :] = gk.astype(BF16)
            tv[place, :] = gv.astype(BF16)

        pair_text(start)

        def keep(j):
            t = 2 * j + 1 - core
            pair = grads(group_of[t] + 2)
            for i in range(2):
                parts[i][t] = pair[i].astype(BF16)
                to_mate(i, j).start()

        def join(j):
            t = 2 * j + core
            pair = grads(group_of[t] + 2)
            for i in range(2):
                await_recv(pair_in.at[i, j], pair_send.at[i, j], pair_recv.at[i, j], mate)
                pair_sum[i, j] = (pair[i] + pair_in[i, j].astype(F32)).astype(BF16)
                pl.when(t != me)(lambda: pair_out(i, j).start())

                @pl.when(t == me)
                def _():
                    got[i, my_head] = pair_sum[i, j]

        keep(chip)
        await_recv(text_in, text_send, text_recv, mate)

        @pl.when(core == 0)
        def _():
            text_sum[...] = (tk[...].astype(F32) + text_in[...].astype(F32)).astype(BF16)

        @pl.when(core == 1)
        def _():
            text_sum[...] = (tv[...].astype(F32) + text_in[...].astype(F32)).astype(BF16)

        cast(mirror, 0).start()
        for n in (1, 2, 3):
            cast(lax.rem(me + 4 * n, NG), n).start()
        text_all[my_head, core] = text_sum[...]

        @pl.loop(1, 8)
        def _(n):
            keep(lax.rem(chip + n, 8))
            join(lax.rem(chip + n - 1, 8))

        join(lax.rem(chip + 7, 8))

    for h in range(NH):
        source = base_of(h) + core

        @pl.when(mirror == source)
        def _():
            await_text(h, core)
            for n in (1, 2, 3):
                pass_on(h, lax.rem(me + 4 * n, NG), relay_send.at[n]).start()

    for h in range(NH):
        source = base_of(h) + core
        pl.when((mirror != source) & (me != source))(lambda: await_text(h, core))
        pass_on(h, mate, mate_send.at[h]).start()

    pl.when(working)(lambda: gq_self().wait())
    acc_q = jnp.zeros((BLK, DH), F32)
    acc_k = jnp.zeros((BLK, DH), F32)
    for h in range(NH):
        cols = slice(h * DH, (h + 1) * DH)
        for i in range(2):
            pl.when(base_of(h) + core != me)(lambda: await_recv(
                got.at[i, h], out_send.at[i, 0], out_recv.at[i, h], base_of(h) + core))
        for p in range(2):
            pl.when(base_of(h) + p != me)(lambda: await_recv(
                got_q.at[2 * h + p], q_send.at[0], q_recv.at[2 * h + p], base_of(h) + p))
            uq[p * HALF:(p + 1) * HALF, cols] = got_q[2 * h + p].astype(F32) * gain_q[:, cols]
        u = got[0, h].astype(F32) * gain_k[:, cols]
        uk[:, cols] = u
        acc_k = acc_k + u * k_ref[:, cols].astype(F32)
        acc_q = acc_q + uq[:, cols] * q_ref[:, cols].astype(F32)
    copies = head_sum(row_sums(acc_q), row_sums(acc_k), sq_send.at[1], sq_recv.at[1], ss.at[1], rs.at[1], hd, nh)
    for h in range(NH):
        cols = slice(h * DH, (h + 1) * DH)
        dv[:, cols] = got[1, h]
    for h in range(NH):
        cols = slice(h * DH, (h + 1) * DH)
        await_text(h, 1 - core)
        dtk[:, cols] = text_all[h, 0]
        dtv[:, cols] = text_all[h, 1]
    inner = head_total(copies, sq_send.at[1], sq_recv.at[1], nh) / (NH * DH * nh)
    cube = scale * scale * scale * inner
    for row, u_ref, x_ref, out in ((0, uq, q_ref, dq), (1, uk, k_ref, dk)):
        col = as_column(scale[row:row + 1])
        col3 = as_column(cube[row:row + 1])
        for h in range(NH):
            cols = slice(h * DH, (h + 1) * DH)
            out[:, cols] = (col * u_ref[:, cols] - x_ref[:, cols].astype(F32) * col3).astype(BF16)

    for h in range(NH):
        source = base_of(h) + core
        pass_on(h, mate, mate_send.at[h]).wait_send()

        @pl.when(mirror == source)
        def _():
            for n in (1, 2, 3):
                pass_on(h, lax.rem(me + 4 * n, NG), relay_send.at[n]).wait_send()

    @pl.when(working)
    def _():
        pair_text(wait_send)
        for n in range(4):
            cast(mate, n).wait_send()

        @pl.loop(0, 8)
        def _(j):
            for i in range(2):
                to_mate(i, j).wait_send()
                pl.when(2 * j + core != me)(lambda: pair_out(i, j).wait_send())

        @pl.loop(1, NG)
        def _(d):
            gq_out(lax.rem(me + d, NG)).wait_send()


def final_kernel(*refs):
    n = 5
    held, sem = refs[2 * n:3 * n], refs[3 * n]
    pieces = [(i, at) for i in range(n) for at in range(0, refs[i].shape[0], BLK)]

    def copy(k, src, dst, way):
        i, at = pieces[k]
        rows = pl.ds(at, BLK)
        return pltpu.make_async_copy(src[i].at[rows], dst[i].at[rows], sem.at[way, k])

    for k in range(len(pieces)):
        copy(k, refs[:n], held, 0).start()
    for k in range(len(pieces)):
        copy(k, refs[:n], held, 0).wait()
        copy(k, held, refs[n:2 * n], 1).start()
    for k in range(len(pieces)):
        copy(k, held, refs[n:2 * n], 1).wait()


VM = pl.BlockSpec(memory_space=pltpu.VMEM)
SM = pl.BlockSpec(memory_space=pltpu.SMEM)
ANY = pl.BlockSpec(memory_space=pl.ANY)
DMA = pltpu.SemaphoreType.DMA


def body(nh, queries, keys, values, text_keys, text_values, d_out, gain_q, gain_k, group_of):
    results = tuple(
        jax.ShapeDtypeStruct((n, NH * DH), BF16) for n in (BLK, BLK, BLK, 2 * BLK, 2 * BLK)
    )
    grads = pl.pallas_call(
        functools.partial(attend_kernel, nh),
        out_shape=results,
        in_specs=[VM] * 4 + [ANY] * 2 + [VM] * 2 + [SM],
        out_specs=(VM,) * 5,
        scratch_shapes=[
            pltpu.VMEM((BLK, NH * DH), BF16),
            pltpu.VMEM((BLK, NH * DH), BF16),
            pltpu.VMEM((NG, BLK, DH), BF16),
            pltpu.VMEM((NG, BLK, DH), BF16),
            pltpu.VMEM((NG, HALF, DH), BF16),
            pltpu.VMEM((NG, HALF, DH), BF16),
            pltpu.VMEM((NP * KC, DH), BF16),
            pltpu.VMEM((NP * KC, DH), BF16),
            pltpu.VMEM((NP, DH, KC), BF16),
            pltpu.VMEM((ROWS, DH), BF16),
            pltpu.VMEM((ROWS, DH), BF16),
            pltpu.VMEM((NP * KC, BLK), F32),
            pltpu.VMEM((NP * KC, BLK), F32),
            [pltpu.VMEM((2 * b + 4, BLK, BLK), BF16) for b in range(NB)],
            [pltpu.VMEM((2 * b + 4, BLK, BLK), BF16) for b in range(NB)],
            pltpu.VMEM((ROWS, DH), F32),
            pltpu.VMEM((NG, HALF, DH), BF16),
            pltpu.VMEM((KC, DH), BF16),
            pltpu.VMEM((KC, DH), BF16),
            pltpu.VMEM((2, 8, BLK, DH), BF16),
            pltpu.VMEM((2, 8, BLK, DH), BF16),
            pltpu.VMEM((2, NH, BLK, DH), BF16),
            pltpu.VMEM((2 * NH, HALF, DH), BF16),
            pltpu.VMEM((2 * BLK, DH), BF16),
            pltpu.VMEM((2 * BLK, DH), BF16),
            pltpu.VMEM((NH, 2, 2 * BLK, DH), BF16),
            pltpu.VMEM((BLK, NH * DH), F32),
            pltpu.VMEM((BLK, NH * DH), F32),
            pltpu.VMEM((2, 8, BLK), F32),
            pltpu.VMEM((2, nh, 8, BLK), F32),
            DMA((4, NG)), DMA((4, NG)), DMA((4, NG)), DMA((4,)), DMA((2,)),
            DMA((2, 8)), DMA((2, 8)), DMA((2, 8)), DMA((2, NH)), DMA((NG,)), DMA((2 * NH,)),
            DMA, DMA, DMA, DMA((4,)), DMA((NH, 2)), DMA((4,)), DMA((NH,)),
            DMA((2, nh)), DMA((2, nh)),
        ],
        compiler_params=pltpu.CompilerParams(
            collective_id=0, has_side_effects=True, vmem_limit_bytes=VMEM_LIMIT
        ),
        name="attend",
    )(queries, keys, values, d_out, text_keys, text_values, gain_q, gain_k, group_of)
    return pl.pallas_call(
        final_kernel,
        out_shape=results,
        in_specs=[ANY] * 5,
        out_specs=(ANY,) * 5,
        scratch_shapes=[pltpu.VMEM(r.shape, BF16) for r in results] + [DMA((2, 7))],
        name="finish",
    )(*grads)


def solution(mesh):
    placed = (
        P("group", "head"),
        P("group", "head"),
        P("group", "head"),
        P(None, "head"),
        P(None, "head"),
        P("group", "head"),
        P("head"),
        P("head"),
        P(),
    )
    return jax.shard_map(
        functools.partial(body, mesh.shape["head"]),
        mesh=mesh,
        in_specs=placed,
        out_specs=(
            P("group", "head"),
            P("group", "head"),
            P("group", "head"),
            P(None, "head"),
            P(None, "head"),
        ),
        check_vma=False,
    )
```

```python
import functools
import math

import jax
import jax.numpy as jnp
from jax import lax
from jax.experimental import pallas as pl
from jax.experimental.pallas import tpu as pltpu
from jax.sharding import PartitionSpec as P

DH = 128
EPS = 1e-06
BLK = 256
NG = 16
NH = 5
HALF = 128
NB = 8
KC = 512
NP = 9
ROWS = 2048
SCALE = DH ** (-0.5)
LOG = SCALE * math.log2(math.e)
MESH = pl.DeviceIdType.MESH
F32 = jnp.float32
BF16 = jnp.bfloat16
VMEM_LIMIT = 62 * 1024 * 1024


def greet(me, hd, nh):
    barrier = pltpu.get_barrier_semaphore()
    for d in range(1, NG):
        pl.semaphore_signal(
            barrier, inc=1, device_id={"group": lax.rem(me + d, NG)}, device_id_type=MESH
        )
    for d in range(1, nh):
        pl.semaphore_signal(
            barrier, inc=1, device_id={"head": lax.rem(hd + d, nh)}, device_id_type=MESH
        )
    return lambda: pl.semaphore_wait(barrier, NG - 1 + nh - 1)


def row_sums(acc):
    return jnp.sum(acc.T, axis=0, keepdims=True)


def as_column(row):
    return jnp.broadcast_to(row, (DH, BLK)).T


def head_sum(row_q, row_k, send, recv, send_sem, recv_sem, hd, nh):
    send[...] = jnp.concatenate([row_q, row_k, jnp.zeros((6, BLK), F32)], axis=0)
    copies = []
    for d in range(1, nh):
        peer = lax.rem(hd + d, nh)
        copy = pltpu.make_async_remote_copy(
            src_ref=send,
            dst_ref=recv.at[d],
            send_sem=send_sem.at[d],
            recv_sem=recv_sem.at[d],
            device_id={"head": peer},
            device_id_type=MESH,
        )
        copy.start()
        copies.append(copy)
    return copies


def head_total(copies, send, recv, nh):
    for copy in copies:
        copy.wait()
    total = send[...]
    for d in range(1, nh):
        total = total + recv[d]
    return total


def base_of(h):
    return 2 * (h + 2 * (h // 3))


def push(src, dst, send_sem, recv_sem, t):
    return pltpu.make_async_remote_copy(
        src_ref=src, dst_ref=dst, send_sem=send_sem, recv_sem=recv_sem,
        device_id={"group": t}, device_id_type=MESH,
    )


def await_recv(dst, send_sem, recv_sem, t):
    push(dst, dst, send_sem, recv_sem, t).wait_recv()


def head_cols(h):
    return pl.ds(pl.multiple_of(h * DH, DH), DH)


def attend_kernel(
    nh, q_ref, k_ref, v_ref, g_ref, tk_ref, tv_ref, gain_q_ref, gain_k_ref, group_of,
    dq, dk, dv, dtk, dtv,
    qn, kn, kall, vall, qall, gall, ks, vs, kt, qs, gs, s_buf, d_buf, p_bufs, ds_bufs, dq_buf, dq_rank,
    tk, tv, pair_in, pair_sum, got, got_q, text_in, text_sum, text_all, uq, uk, sq_send, sq_recv,
    in_send, in_recv, relay_sem, local_sem, text_sem,
    pair_send, pair_recv, out_send, out_recv, q_send, q_recv, q_local,
    text_send, text_recv, cast_send, cast_recv, relay_send, mate_send, ss, rs,
):
    me = lax.axis_index("group")
    hd = lax.axis_index("head")
    core = lax.rem(me, 2)
    mate = me + 1 - 2 * core
    mirror = me + 2 - 4 * lax.rem(lax.div(me, 2), 2)
    chip = lax.div(me, 2)
    my_head = chip - 2 * lax.div(chip, 5)
    working = (chip < 3) | (chip == 5) | (chip == 6)
    gain_q = gain_q_ref[...].astype(F32)[None, :]
    gain_k = gain_k_ref[...].astype(F32)[None, :]

    def text_copy(i):
        return pltpu.make_async_copy(
            (tk_ref, tv_ref)[i].at[:, head_cols(my_head)], (ks, vs)[i].at[pl.ds(0, KC)],
            text_sem.at[i])

    pl.when(working)(lambda: [text_copy(i).start() for i in range(2)] and None)
    met = greet(me, hd, nh)

    whole = ((0, v_ref, vall), (2, kn, kall))
    halves = ((1, g_ref, gall), (3, qn, qall))

    def half_src(ref, h, part):
        return ref.at[pl.ds(pl.multiple_of(part * HALF, HALF), HALF), head_cols(h)]

    def to_all(stage, act):
        kind, ref, out = whole[stage]
        kind2, ref2, out2 = halves[stage]

        @pl.loop(0, NH)
        def _(d):
            h = lax.rem(my_head + 1 + d, NH)
            base = 2 * (h + 2 * lax.div(h, 3))

            @pl.when(base + core != me)
            def _():
                act(push(ref.at[:, head_cols(h)], out.at[me],
                         in_send.at[kind, 2 * h + core], in_recv.at[kind, me], base + core))

            for part in range(2):
                @pl.when(base + part != me)
                def _():
                    act(push(half_src(ref2, h, part), out2.at[me],
                             in_send.at[kind2, 2 * h + part], in_recv.at[kind2, me], base + part))

    def to_self(stage, act):
        kind, ref, out = whole[stage]
        kind2, ref2, out2 = halves[stage]

        @pl.when(working)
        def _():
            act(pltpu.make_async_copy(
                ref.at[:, head_cols(my_head)], out.at[me], local_sem.at[kind]))
            act(pltpu.make_async_copy(
                half_src(ref2, my_head, core), out2.at[me], local_sem.at[kind2]))

    def start(copy):
        copy.start()

    def relay(stage, s):
        kind, ref, out = whole[stage]
        view = out.at[s]
        return push(view, view, relay_sem.at[kind, s], in_recv.at[kind, s], mate)

    def relay_all(stage):
        kind, ref, out = whole[stage]

        @pl.when(working)
        def _():
            relay(stage, me).start()

            @pl.loop(1, 8)
            def _(d):
                s = lax.rem(me + NG - 2 * d, NG)
                await_recv(out.at[s], in_send.at[kind, 0], in_recv.at[kind, s], s)
                relay(stage, s).start()

    acc_q = jnp.zeros((BLK, DH), F32)
    acc_k = jnp.zeros((BLK, DH), F32)
    for h in range(NH):
        cols = slice(h * DH, (h + 1) * DH)
        x = q_ref[:, cols].astype(F32)
        acc_q = acc_q + x * x
        x = k_ref[:, cols].astype(F32)
        acc_k = acc_k + x * x
    sums = row_sums(acc_q), row_sums(acc_k)
    order = [
        jnp.minimum(
            sum((group_of[t] == r).astype(jnp.int32) * t for t in range(1, NG)), NG - 1)
        for r in range(NG)
    ]
    met()
    copies = head_sum(*sums, sq_send.at[0], sq_recv.at[0], ss.at[0], rs.at[0], hd, nh)
    to_all(0, start)
    to_self(0, start)
    total = head_total(copies, sq_send.at[0], sq_recv.at[0], nh)
    scale = lax.rsqrt(total / (NH * DH * nh) + EPS)
    col_q = as_column(scale[0:1])
    col_k = as_column(scale[1:2])
    for h in range(NH):
        cols = slice(h * DH, (h + 1) * DH)
        kn[:, cols] = (k_ref[:, cols].astype(F32) * col_k * gain_k[:, cols]).astype(BF16)
        qn[:, cols] = (q_ref[:, cols].astype(F32) * col_q * gain_q[:, cols]).astype(BF16)
    to_all(1, start)
    to_self(1, start)

    to_self(0, lambda copy: copy.wait())
    relay_all(0)
    to_self(1, lambda copy: copy.wait())
    relay_all(1)

    @pl.when(working)
    def _():
        @pl.loop(1, NG)
        def _(d):
            s = lax.rem(me + d, NG)

            @pl.when(lax.rem(d, 2) == 1)
            def _():
                for kind, ref, out in whole:
                    await_recv(out.at[s], in_send.at[kind, 0], in_recv.at[kind, s], s)

            for kind, ref, out in halves:
                await_recv(out.at[s], in_send.at[kind, 0], in_recv.at[kind, s], s)

    @pl.when(working)
    def _():
        for i in range(2):
            text_copy(i).wait()

        for r in range(NG):
            qs[r * HALF:(r + 1) * HALF, :] = qall[order[r]]
            gs[r * HALF:(r + 1) * HALF, :] = gall[order[r]]
        for r in range(NG):
            ks[(r + 2) * BLK:(r + 3) * BLK, :] = kall[order[r]]
            vs[(r + 2) * BLK:(r + 3) * BLK, :] = vall[order[r]]
        for i in range(NP):
            kt[i] = ks[i * KC:(i + 1) * KC, :].T

        def fold(x, op):
            return op(x.reshape(x.shape[0] // 8, 8, x.shape[-1]), axis=0)

        def rows_block(b):
            n = b + 2
            rows = slice(b * BLK, (b + 1) * BLK)
            q_cols = qs[rows, :].T
            g_cols = gs[rows, :].T
            later = lax.broadcasted_iota(jnp.int32, (1, BLK), 1) >= HALF
            at = [slice(i * KC, (i + 1) * KC) for i in range(n)]
            top = jnp.full((1, BLK), -jnp.inf, F32)
            norm = jnp.zeros((8, BLK), F32)
            inner = jnp.zeros((8, BLK), F32)
            tops = []
            for i in range(n):
                s = jnp.dot(ks[at[i], :], q_cols, preferred_element_type=F32)
                dp = jnp.dot(vs[at[i], :], g_cols, preferred_element_type=F32)
                if i == n - 1:
                    s = jnp.concatenate([s[0:BLK], jnp.where(later, s[BLK:KC], -jnp.inf)], axis=0)
                new = jnp.maximum(top, jnp.max(fold(s, jnp.max), axis=0, keepdims=True) * LOG)
                e = jnp.exp2(s * LOG - new)
                s_buf[at[i], :] = e
                d_buf[at[i], :] = dp
                shrink = jnp.exp2(top - new)
                norm = norm * shrink + fold(e, jnp.sum)
                inner = inner * shrink + fold(e * dp, jnp.sum)
                top = new
                tops.append(new)
            inv = 1.0 / jnp.sum(norm, axis=0, keepdims=True)
            delta = jnp.sum(inner, axis=0, keepdims=True) * inv
            dq = jnp.zeros((DH, BLK), F32)
            for i in range(n):
                p = s_buf[at[i], :] * (jnp.exp2(tops[i] - top) * inv)
                ds = (p * (d_buf[at[i], :] - delta)).astype(BF16)
                soft = p.astype(BF16)
                for j in range(2):
                    p_bufs[b][2 * i + j] = soft[j * BLK:(j + 1) * BLK]
                    ds_bufs[b][2 * i + j] = ds[j * BLK:(j + 1) * BLK]
                dq = dq + jnp.dot(kt[i], ds, preferred_element_type=F32)
            dq_buf[rows, :] = dq.T * SCALE

        for b in range(NB):
            rows_block(b)

    @pl.when(working)
    def _():
        @pl.loop(0, 8)
        def _(d):
            s = lax.rem(me + 2 * d, NG)
            for stage in range(2):
                relay(stage, s).wait_send()

    for stage in range(2):
        to_all(stage, lambda copy: copy.wait_send())

    parts = (kall, vall)
    texts = (tk, tv)

    def wait_send(copy):
        copy.wait_send()

    def to_mate(i, j):
        return push(parts[i].at[2 * j + 1 - core], pair_in.at[i, j],
                    pair_send.at[i, j], pair_recv.at[i, j], mate)

    def text_to(i):
        return push(texts[i], text_in, text_send, text_recv, mate)

    def gq_out(t):
        return push(qall.at[t], got_q.at[2 * my_head + core],
                    q_send.at[t], q_recv.at[2 * my_head + core], t)

    def gq_self():
        return pltpu.make_async_copy(qall.at[me], got_q.at[2 * my_head + core], q_local)

    def pair_out(i, j):
        return push(pair_sum.at[i, j], got.at[i, my_head],
                    out_send.at[i, j], out_recv.at[i, my_head], 2 * j + core)

    def cast(t, n):
        return push(text_sum, text_all.at[my_head, core],
                    cast_send.at[n], cast_recv.at[my_head, core], t)

    def pass_on(h, t, sem):
        view = text_all.at[h, core]
        return push(view, view, sem, cast_recv.at[h, core], t)

    def await_text(h, kind):
        view = text_all.at[h, kind]
        await_recv(view, cast_send.at[0], cast_recv.at[h, kind], mate)

    def pair_text(act):
        pl.when(core == 0)(lambda: act(text_to(1)))
        pl.when(core == 1)(lambda: act(text_to(0)))

    def grads(chunk):
        gk = gv = 0
        for b in range(NB):
            rows = slice(b * BLK, (b + 1) * BLK)
            last = 2 * b + 3
            index = jnp.minimum(chunk, last)
            here_k = jnp.dot(ds_bufs[b][index], qs[rows, :], preferred_element_type=F32)
            here_v = jnp.dot(p_bufs[b][index], gs[rows, :], preferred_element_type=F32)
            if b < NB - 1:
                seen = (chunk <= last).astype(F32)
                here_k, here_v = here_k * seen, here_v * seen
            gk, gv = gk + here_k, gv + here_v
        return gk * SCALE, gv

    @pl.when(working)
    def _():
        for r in range(NG):
            dq_rank[r] = dq_buf[r * HALF:(r + 1) * HALF, :].astype(BF16)
        for s in range(NG):
            qall[s] = dq_rank[group_of[s]]

        @pl.loop(1, NG)
        def _(d):
            gq_out(lax.rem(me + d, NG)).start()

        gq_self().start()

        @pl.loop(0, 2)
        def _(i):
            gk, gv = grads(i)
            place = pl.ds(pl.multiple_of(i * BLK, BLK), BLK)
            tk[place, :] = gk.astype(BF16)
            tv[place, :] = gv.astype(BF16)

        pair_text(start)

        def keep(j):
            t = 2 * j + 1 - core
            pair = grads(group_of[t] + 2)
            for i in range(2):
                parts[i][t] = pair[i].astype(BF16)
                to_mate(i, j).start()

        def join(j):
            t = 2 * j + core
            pair = grads(group_of[t] + 2)
            for i in range(2):
                await_recv(pair_in.at[i, j], pair_send.at[i, j], pair_recv.at[i, j], mate)
                pair_sum[i, j] = (pair[i] + pair_in[i, j].astype(F32)).astype(BF16)
                pl.when(t != me)(lambda: pair_out(i, j).start())

                @pl.when(t == me)
                def _():
                    got[i, my_head] = pair_sum[i, j]

        keep(chip)
        await_recv(text_in, text_send, text_recv, mate)

        @pl.when(core == 0)
        def _():
            text_sum[...] = (tk[...].astype(F32) + text_in[...].astype(F32)).astype(BF16)

        @pl.when(core == 1)
        def _():
            text_sum[...] = (tv[...].astype(F32) + text_in[...].astype(F32)).astype(BF16)

        cast(mirror, 0).start()
        for n in (1, 2, 3):
            cast(lax.rem(me + 4 * n, NG), n).start()
        text_all[my_head, core] = text_sum[...]

        @pl.loop(1, 8)
        def _(n):
            keep(lax.rem(chip + n, 8))
            join(lax.rem(chip + n - 1, 8))

        join(lax.rem(chip + 7, 8))

    for h in range(NH):
        source = base_of(h) + core

        @pl.when(mirror == source)
        def _():
            await_text(h, core)
            for n in (1, 2, 3):
                pass_on(h, lax.rem(me + 4 * n, NG), relay_send.at[n]).start()

    for h in range(NH):
        source = base_of(h) + core
        pl.when((mirror != source) & (me != source))(lambda: await_text(h, core))
        pass_on(h, mate, mate_send.at[h]).start()

    pl.when(working)(lambda: gq_self().wait())
    acc_q = jnp.zeros((BLK, DH), F32)
    acc_k = jnp.zeros((BLK, DH), F32)
    for h in range(NH):
        cols = slice(h * DH, (h + 1) * DH)
        for i in range(2):
            pl.when(base_of(h) + core != me)(lambda: await_recv(
                got.at[i, h], out_send.at[i, 0], out_recv.at[i, h], base_of(h) + core))
        for p in range(2):
            pl.when(base_of(h) + p != me)(lambda: await_recv(
                got_q.at[2 * h + p], q_send.at[0], q_recv.at[2 * h + p], base_of(h) + p))
            uq[p * HALF:(p + 1) * HALF, cols] = got_q[2 * h + p].astype(F32) * gain_q[:, cols]
        u = got[0, h].astype(F32) * gain_k[:, cols]
        uk[:, cols] = u
        acc_k = acc_k + u * k_ref[:, cols].astype(F32)
        acc_q = acc_q + uq[:, cols] * q_ref[:, cols].astype(F32)
    copies = head_sum(row_sums(acc_q), row_sums(acc_k), sq_send.at[1], sq_recv.at[1], ss.at[1], rs.at[1], hd, nh)
    for h in range(NH):
        cols = slice(h * DH, (h + 1) * DH)
        dv[:, cols] = got[1, h]
    for h in range(NH):
        cols = slice(h * DH, (h + 1) * DH)
        await_text(h, 1 - core)
        dtk[:, cols] = text_all[h, 0]
        dtv[:, cols] = text_all[h, 1]
    inner = head_total(copies, sq_send.at[1], sq_recv.at[1], nh) / (NH * DH * nh)
    cube = scale * scale * scale * inner
    for row, u_ref, x_ref, out in ((0, uq, q_ref, dq), (1, uk, k_ref, dk)):
        col = as_column(scale[row:row + 1])
        col3 = as_column(cube[row:row + 1])
        for h in range(NH):
            cols = slice(h * DH, (h + 1) * DH)
            out[:, cols] = (col * u_ref[:, cols] - x_ref[:, cols].astype(F32) * col3).astype(BF16)

    for h in range(NH):
        source = base_of(h) + core
        pass_on(h, mate, mate_send.at[h]).wait_send()

        @pl.when(mirror == source)
        def _():
            for n in (1, 2, 3):
                pass_on(h, lax.rem(me + 4 * n, NG), relay_send.at[n]).wait_send()

    @pl.when(working)
    def _():
        pair_text(wait_send)
        for n in range(4):
            cast(mate, n).wait_send()

        @pl.loop(0, 8)
        def _(j):
            for i in range(2):
                to_mate(i, j).wait_send()
                pl.when(2 * j + core != me)(lambda: pair_out(i, j).wait_send())

        @pl.loop(1, NG)
        def _(d):
            gq_out(lax.rem(me + d, NG)).wait_send()


def final_kernel(*refs):
    n = 5
    held, sem = refs[2 * n:3 * n], refs[3 * n]
    pieces = [(i, at) for i in range(n) for at in range(0, refs[i].shape[0], BLK)]

    def copy(k, src, dst, way):
        i, at = pieces[k]
        rows = pl.ds(at, BLK)
        return pltpu.make_async_copy(src[i].at[rows], dst[i].at[rows], sem.at[way, k])

    for k in range(len(pieces)):
        copy(k, refs[:n], held, 0).start()
    for k in range(len(pieces)):
        copy(k, refs[:n], held, 0).wait()
        copy(k, held, refs[n:2 * n], 1).start()
    for k in range(len(pieces)):
        copy(k, held, refs[n:2 * n], 1).wait()


VM = pl.BlockSpec(memory_space=pltpu.VMEM)
SM = pl.BlockSpec(memory_space=pltpu.SMEM)
ANY = pl.BlockSpec(memory_space=pl.ANY)
DMA = pltpu.SemaphoreType.DMA


def body(nh, queries, keys, values, text_keys, text_values, d_out, gain_q, gain_k, group_of):
    results = tuple(
        jax.ShapeDtypeStruct((n, NH * DH), BF16) for n in (BLK, BLK, BLK, 2 * BLK, 2 * BLK)
    )
    grads = pl.pallas_call(
        functools.partial(attend_kernel, nh),
        out_shape=results,
        in_specs=[VM] * 4 + [ANY] * 2 + [VM] * 2 + [SM],
        out_specs=(VM,) * 5,
        scratch_shapes=[
            pltpu.VMEM((BLK, NH * DH), BF16),
            pltpu.VMEM((BLK, NH * DH), BF16),
            pltpu.VMEM((NG, BLK, DH), BF16),
            pltpu.VMEM((NG, BLK, DH), BF16),
            pltpu.VMEM((NG, HALF, DH), BF16),
            pltpu.VMEM((NG, HALF, DH), BF16),
            pltpu.VMEM((NP * KC, DH), BF16),
            pltpu.VMEM((NP * KC, DH), BF16),
            pltpu.VMEM((NP, DH, KC), BF16),
            pltpu.VMEM((ROWS, DH), BF16),
            pltpu.VMEM((ROWS, DH), BF16),
            pltpu.VMEM((NP * KC, BLK), F32),
            pltpu.VMEM((NP * KC, BLK), F32),
            [pltpu.VMEM((2 * b + 4, BLK, BLK), BF16) for b in range(NB)],
            [pltpu.VMEM((2 * b + 4, BLK, BLK), BF16) for b in range(NB)],
            pltpu.VMEM((ROWS, DH), F32),
            pltpu.VMEM((NG, HALF, DH), BF16),
            pltpu.VMEM((KC, DH), BF16),
            pltpu.VMEM((KC, DH), BF16),
            pltpu.VMEM((2, 8, BLK, DH), BF16),
            pltpu.VMEM((2, 8, BLK, DH), BF16),
            pltpu.VMEM((2, NH, BLK, DH), BF16),
            pltpu.VMEM((2 * NH, HALF, DH), BF16),
            pltpu.VMEM((2 * BLK, DH), BF16),
            pltpu.VMEM((2 * BLK, DH), BF16),
            pltpu.VMEM((NH, 2, 2 * BLK, DH), BF16),
            pltpu.VMEM((BLK, NH * DH), F32),
            pltpu.VMEM((BLK, NH * DH), F32),
            pltpu.VMEM((2, 8, BLK), F32),
            pltpu.VMEM((2, nh, 8, BLK), F32),
            DMA((4, NG)), DMA((4, NG)), DMA((4, NG)), DMA((4,)), DMA((2,)),
            DMA((2, 8)), DMA((2, 8)), DMA((2, 8)), DMA((2, NH)), DMA((NG,)), DMA((2 * NH,)),
            DMA, DMA, DMA, DMA((4,)), DMA((NH, 2)), DMA((4,)), DMA((NH,)),
            DMA((2, nh)), DMA((2, nh)),
        ],
        compiler_params=pltpu.CompilerParams(
            collective_id=0, has_side_effects=True, vmem_limit_bytes=VMEM_LIMIT
        ),
        name="attend",
    )(queries, keys, values, d_out, text_keys, text_values, gain_q, gain_k, group_of)
    return pl.pallas_call(
        final_kernel,
        out_shape=results,
        in_specs=[ANY] * 5,
        out_specs=(ANY,) * 5,
        scratch_shapes=[pltpu.VMEM(r.shape, BF16) for r in results] + [DMA((2, 7))],
        name="finish",
    )(*grads)


def solution(mesh):
    placed = (
        P("group", "head"),
        P("group", "head"),
        P("group", "head"),
        P(None, "head"),
        P(None, "head"),
        P("group", "head"),
        P("head"),
        P("head"),
        P(),
    )
    return jax.shard_map(
        functools.partial(body, mesh.shape["head"]),
        mesh=mesh,
        in_specs=placed,
        out_specs=(
            P("group", "head"),
            P("group", "head"),
            P("group", "head"),
            P(None, "head"),
            P(None, "head"),
        ),
        check_vma=False,
    )
```
